32 devices in a mesh: dp: 16 (over z, y, x), context: 2 (over core).
Axes of the slice: x: 2, y: 2, z: 4, core: 2. Of those that a mesh axis runs over, the one named last changes fastest.
Arguments:
- hidden_in: bfloat16 [16, 256, 2048], P('dp', 'context'), may hold values from -6 to 6
- cotangent: bfloat16 [16, 256, 2048], P('dp', 'context'), may hold values from -6 to 6
- tile_depth: int32 [16, 2], P('dp'), may hold values from 1 to 4, as said below
- w_qkv: bfloat16 [3, 2048, 256], P(None, 'dp', 'context'), may hold values from -0.125 to 0.125
- w_out: bfloat16 [256, 2048], P('context', 'dp'), may hold values from -0.375 to 0.375
- gain: float32 [2048], replicated, may hold values from 0.1 to 1.9
Outputs:
- hidden_out: bfloat16 [16, 256, 2048], P('dp', 'context')
- grad_in: bfloat16 [16, 256, 2048], P('dp', 'context')
- grad_qkv: float32 [3, 2048, 256], P(None, 'dp', 'context')
- grad_out: float32 [256, 2048], P('context', 'dp')
The draws below stay inside these ranges and needn't reach their ends.
Inputs may be any that keep to these rules, and one draw needn't show every extreme that they name: `tile_depth`: in every document at most 1 tiles have depth 2 or more and at most 1 have depth 3 or more; some document has exactly 1 and 1 such tiles.
All inputs are finite; a program needn't handle non-finite values.
Results may differ from the reference program's by a relative error of at most 0.028.
Values may be sent and summed in bfloat16 or wider, within the bound.
A program may use at most 64 MiB of HBM per device.

```python
import jax
import jax.numpy as jnp
from jax import lax

D = 2048
HD = 128
HEAD_DEV = 1
TILE = 128
HEADS = 2
INNER = 256
TILES_DOC = 2
SEQ = 256
DOCS = 16
CAP2 = 1
CAP3 = 1
N_CONTEXT = 2


def draw_tile_depth(key, part):
    key = jax.random.fold_in(key, 7)
    keys = jax.random.split(key, 5)
    docs = jnp.arange(DOCS)
    many2 = jax.random.randint(keys[0], (DOCS,), 0, CAP2 + 1)
    many3 = jnp.minimum(jax.random.randint(keys[1], (DOCS,), 0, CAP3 + 1), many2)
    chosen = jax.random.randint(keys[2], (), 0, DOCS)
    many2 = jnp.where(docs == chosen, CAP2, many2)
    many3 = jnp.where(docs == chosen, CAP3, many3)
    orders = jax.vmap(lambda k: jax.random.permutation(k, TILES_DOC))(jax.random.split(keys[3], DOCS))
    rank = jnp.argsort(orders, axis=-1, stable=True).astype(jnp.int32)
    extra = jax.random.randint(keys[4], (DOCS, TILES_DOC), 0, 2)
    extra = jnp.where((docs[:, None] == chosen) & (rank == 0), 1, extra)
    deep2 = (rank < many2[:, None]).astype(jnp.int32)
    deep3 = (rank < many3[:, None]).astype(jnp.int32)
    return (1 + deep2 + deep3 * (1 + extra)).astype(jnp.int32)


def shard_levels(own_key, dims, cuts, smallest, high):
    level, own = 1.0, jax.random.fold_in(own_key, 6)
    for dim, blocks in cuts:
        draws = jnp.exp(jax.random.uniform(jax.random.fold_in(own, dim), (blocks,), jnp.float32, smallest / len(cuts), high / len(cuts)))
        level = level * jnp.repeat(draws, dims[dim] // blocks).reshape([-1 if axis == dim else 1 for axis in range(len(dims))])
    return level


def bell_draw(stream_key, dims, scale, limit, cuts=(), held_as=jnp.bfloat16):
    entries = scale * jax.random.normal(stream_key, dims, jnp.float32)
    if cuts:
        entries = entries * shard_levels(stream_key, dims, cuts, -0.22, 0.18)
    return jnp.clip(entries, -limit, limit).astype(held_as)


def setup_inputs(seed: int = 0) -> dict:
    splits = jax.random.split(jax.random.key(seed), 7)
    return {
        "hidden_in": bell_draw(splits[0], (DOCS, SEQ, D), 1.0, 6.0, ((0, 16), (1, 2))),
        "cotangent": bell_draw(splits[1], (DOCS, SEQ, D), 1.0, 6.0, ((0, 16), (1, 2))),
        "tile_depth": draw_tile_depth(jax.random.fold_in(splits[6], 71), 0),
        "w_qkv": bell_draw(splits[3], (3, D, INNER), D ** -0.5, 0.125, ((1, 16), (2, 2))),
        "w_out": bell_draw(splits[4], (INNER, D), INNER ** -0.5, 0.375, ((0, 2), (1, 16))),
        "gain": jnp.clip(1.0 + 0.18 * jax.random.normal(splits[5], (D,), jnp.float32), 0.1, 1.9),
    }


def norm_rows(x32, gain):
    inv = lax.rsqrt(lax.optimization_barrier(jnp.mean(x32 * x32, -1, keepdims=True)) + 1e-06)
    return (inv, (x32 * inv * gain).astype(jnp.bfloat16))

def slot_plan(depth, level, cap):
    alive = depth >= level
    alive_int = alive.astype(jnp.int32)
    rank = (jnp.cumsum(alive_int) - alive_int).astype(jnp.int32)
    places = jnp.arange(depth.shape[0], dtype=jnp.int32)
    owners = jnp.stack([jnp.sum(jnp.where(alive & (rank == s), places, 0)) for s in range(cap)]).astype(jnp.int32)
    valid = jnp.stack([jnp.any(alive & (rank == s)) for s in range(cap)])
    return (alive, jnp.minimum(rank, cap - 1).astype(jnp.int32), owners, valid)

def collect(tiles, owners, valid):
    picked = jnp.take(tiles, owners, axis=0)
    picked = jnp.where(valid[:, None, None], picked, jnp.zeros_like(picked))
    return picked.reshape(-1, tiles.shape[-1])

def spread(rows, rank, alive, tile):
    per_slot = rows.reshape(-1, tile, rows.shape[-1])
    back = jnp.take(per_slot, rank, axis=0)
    return jnp.where(alive[:, None, None], back, jnp.zeros_like(back))

def group_round(terms):
    rounded = lax.optimization_barrier(terms.astype(jnp.bfloat16)).astype(jnp.float32)
    return lax.optimization_barrier(jnp.sum(rounded, 0))

def doc_pass(carry, inputs):
    w_qkv, w_out, gain, acc_qkv, acc_out = carry
    hidden, grad, depth = inputs
    scale = HD ** (-0.5)
    state = hidden.reshape(N_CONTEXT, TILE, D)
    saved = []
    for level, cap in ((2, CAP2), (3, CAP3)):
        alive, rank, owners, valid = slot_plan(depth, level, cap)
        x32 = state.astype(jnp.float32)
        inv, normed = norm_rows(x32, gain)
        rows = collect(normed, owners, valid)
        count = rows.shape[0]
        qkv = jnp.einsum('rd,tdc->trc', rows.astype(jnp.float32), w_qkv.astype(jnp.float32)).astype(jnp.bfloat16)
        heads = qkv.reshape(3, count, HEADS, HD)
        query, key, value = (heads[0], heads[1], heads[2])
        valid_rows = jnp.repeat(valid, TILE)
        pos = jnp.arange(count)
        allowed = valid_rows[None, :] & (pos[None, :] <= pos[:, None])
        scores = jnp.einsum('qhd,khd->hqk', query.astype(jnp.float32), key.astype(jnp.float32)) * scale
        scores = jnp.where(allowed[None], scores, -1e+30)
        top = lax.optimization_barrier(jnp.max(scores, -1, keepdims=True))
        expo = jnp.exp(scores - top)
        prob = expo / lax.optimization_barrier(jnp.sum(expo, -1, keepdims=True))
        probb = prob.astype(jnp.bfloat16)
        attn = jnp.einsum('hqk,khd->qhd', probb.astype(jnp.float32), value.astype(jnp.float32)).astype(jnp.bfloat16)
        attn_flat = attn.reshape(count, INNER)
        groups = attn_flat.reshape(count, N_CONTEXT, HEAD_DEV * HD).astype(jnp.float32)
        w_groups = w_out.reshape(N_CONTEXT, HEAD_DEV * HD, D).astype(jnp.float32)
        mixed = group_round(jnp.einsum('rgc,gcd->grd', groups, w_groups))
        state = (x32 + spread(mixed, rank, alive, TILE)).astype(jnp.bfloat16)
        saved.append((alive, rank, owners, valid, x32, inv, rows, query, key, value, prob, probb, attn, attn_flat))
    hidden_out = state.reshape(SEQ, D)
    gstate = grad.reshape(N_CONTEXT, TILE, D)
    for index in (1, 0):
        alive, rank, owners, valid, x32, inv, rows, query, key, value, prob, probb, attn, attn_flat = saved[index]
        count = rows.shape[0]
        masked = jnp.where(alive[:, None, None], gstate, jnp.zeros_like(gstate))
        dy = collect(masked, owners, valid)
        dattn = jnp.dot(dy, w_out.T, preferred_element_type=jnp.float32).astype(jnp.bfloat16)
        acc_out = acc_out + jnp.dot(attn_flat.T, dy, preferred_element_type=jnp.float32)
        dheads = dattn.reshape(count, HEADS, HD).astype(jnp.float32)
        delta = lax.optimization_barrier(jnp.sum(dheads * attn.astype(jnp.float32), -1))
        dprob = jnp.einsum('qhd,khd->hqk', dheads, value.astype(jnp.float32))
        dscore = (prob * (dprob - delta.T[:, :, None]) * scale).astype(jnp.bfloat16).astype(jnp.float32)
        dq = jnp.einsum('hqk,khd->qhd', dscore, key.astype(jnp.float32)).astype(jnp.bfloat16)
        dk = jnp.einsum('hqk,qhd->khd', dscore, query.astype(jnp.float32)).astype(jnp.bfloat16)
        dv = jnp.einsum('hqk,qhd->khd', probb.astype(jnp.float32), dheads).astype(jnp.bfloat16)
        dqkv = jnp.stack([dq, dk, dv]).reshape(3, count, INNER).astype(jnp.float32)
        acc_qkv = acc_qkv + jnp.einsum('rd,trc->tdc', rows.astype(jnp.float32), dqkv)
        dgroups = dqkv.reshape(3, count, N_CONTEXT, HEAD_DEV * HD)
        wq_groups = w_qkv.reshape(3, D, N_CONTEXT, HEAD_DEV * HD).astype(jnp.float32)
        dnorm = group_round(jnp.einsum('trgc,tdgc->grd', dgroups, wq_groups))
        back = spread(dnorm, rank, alive, TILE)
        scaled = back * gain
        dx = inv * scaled - x32 * inv ** 3 * lax.optimization_barrier(jnp.mean(x32 * scaled, -1, keepdims=True))
        dx = jnp.where(alive[:, None, None], dx, jnp.zeros_like(dx))
        gstate = (gstate.astype(jnp.float32) + dx).astype(jnp.bfloat16)
    return ((w_qkv, w_out, gain, acc_qkv, acc_out), (hidden_out, gstate.reshape(SEQ, D)))

def reference(hidden_in, cotangent, tile_depth, w_qkv, w_out, gain):
    start = (w_qkv, w_out, gain, jnp.zeros((3, D, INNER), jnp.float32), jnp.zeros((INNER, D), jnp.float32))
    carry, outs = lax.scan(doc_pass, start, (hidden_in, cotangent, tile_depth))
    return (outs[0], outs[1], carry[3], carry[4])
```

```python
import functools

import jax
import jax.numpy as jnp
from jax import lax
from jax.experimental import pallas as pl
from jax.experimental.pallas import tpu as pltpu
from jax.sharding import PartitionSpec as P

HD = 128
MESH = pl.DeviceIdType.MESH
BF = jnp.bfloat16
F32 = jnp.float32
EXCHANGES = ("mix2", "mix3", "dn3", "dn2")


def grid_of(n):
    if n == 64:
        return (16, 4, 1)
    if n % 4 == 0:
        return (n // 4, 2, 2)
    return (n, 1, 1)


def copy_keys(dims, contexts, chunks):
    Z, Y, X = dims
    first = (X, Y)
    second = (Y, X)
    keys = []
    for o in range(1, contexts):
        keys += [("hid", o), ("cot", o)]
        keys += [(name, o, j) for name in EXCHANGES for j in range(chunks)]
    for h in range(2):
        keys += [("gz", h, oz) for oz in range(1, Z)]
        keys += [("g1", h, o1, oz) for o1 in range(1, first[h]) for oz in range(Z)]
        keys += [
            ("g2", h, o2, o1, oz)
            for o2 in range(1, second[h])
            for o1 in range(first[h])
            for oz in range(Z)
        ]
        keys += [
            ("s1", h, o1, o2, oz)
            for o1 in range(1, second[h])
            for o2 in range(first[h])
            for oz in range(Z)
        ]
        keys += [("s2", h, o2, oz) for o2 in range(1, first[h]) for oz in range(Z)]
        keys += [("s3", h, oz) for oz in range(1, Z)]
    return {key: number for number, key in enumerate(keys)}


def nn(a, b):
    return jnp.dot(a, b, preferred_element_type=F32)


def nt(a, b):
    return lax.dot_general(a, b, (((1,), (1,)), ((), ())), preferred_element_type=F32)


def kernel(
    dims, contexts, chunks, keys,
    depth, hid, cot, wq, wo, gain,
    hout, gout, gqkv, gwo,
    WA, WB, WAT, WBT, accA, accB, peer_h, peer_g, hL, h2, R, DY, scaled, own_x, got_x,
    G, R1a, R1b, R2a, R2b, R3, T1a, T1b, T2, send_sem, recv_sem,
):
    Z, Y, X = dims
    dp = lax.axis_index("dp")
    ctx = lax.axis_index("context")
    zz, yy, xx = dp // (Y * X), lax.rem(dp // X, Y), lax.rem(dp, X)
    tile, D = hid.shape[1], hid.shape[2]
    dloc = wq.shape[1]
    width = D // chunks
    me = (zz, yy, xx)
    order = ((2, 1), (1, 2))

    def spot(**moves):
        place = list(me)
        for name, off in moves.items():
            axis = int(name[1])
            place[axis] = lax.rem(me[axis] + off + dims[axis], dims[axis]) if off else me[axis]
        return (place[0] * Y + place[1]) * X + place[2]

    def at(axes):
        return spot(**{"a%d" % axis: off for axis, off in axes})

    started = []

    def copy(key, src, dst, peer):
        number = keys[key]
        return pltpu.make_async_remote_copy(
            src_ref=src, dst_ref=dst, send_sem=send_sem.at[number], recv_sem=recv_sem.at[number],
            device_id=peer, device_id_type=MESH,
        )

    def send(key, src, dst, peer):
        c = copy(key, src, dst, peer)
        c.start()
        started.append(c)

    def arrive(key, dst):
        copy(key, dst, dst, (dp, ctx)).wait_recv()

    def ctx_peer(o):
        return (dp, lax.rem(ctx + o, contexts))

    barrier = pltpu.get_barrier_semaphore()
    peers = [(at([(axis, o)]), ctx) for axis in range(3) for o in range(1, dims[axis])]
    peers += [ctx_peer(o) for o in range(1, contexts)]
    for peer in peers:
        pl.semaphore_signal(barrier, inc=1, device_id=peer, device_id_type=MESH)

    mine = pl.ds(pl.multiple_of(dp * dloc, dloc), dloc)
    WA[mine, 0:HD] = wq[0]
    WA[mine, HD : 2 * HD] = wq[1]
    WB[mine, 0:HD] = wq[2]
    WB[mine, HD : 2 * HD] = wo[...].T
    pl.semaphore_wait(barrier, len(peers))

    halves = (WA, WB)

    def piece(h, axes):
        p = at(axes)
        return halves[h].at[pl.ds(pl.multiple_of(p * dloc, dloc), dloc), :]

    for h in range(2):
        for oz in range(1, Z):
            block = piece(h, [])
            send(("gz", h, oz), block, block, (at([(0, oz)]), ctx))
    for o in range(1, contexts):
        slot = contexts - o - 1
        send(("hid", o), hid.at[0], peer_h.at[slot], ctx_peer(o))
        send(("cot", o), cot.at[0], peer_g.at[slot], ctx_peer(o))

    def spread_first(h, oz):
        d1 = order[h][0]
        block = piece(h, [(0, -oz)])
        for o1 in range(1, dims[d1]):
            send(("g1", h, o1, oz), block, block, (at([(d1, o1)]), ctx))

    def spread_second(h, oz, o1):
        d1, d2 = order[h]
        block = piece(h, [(0, -oz), (d1, -o1)])
        if o1:
            arrive(("g1", h, o1, oz), block)
        for o2 in range(1, dims[d2]):
            send(("g2", h, o2, o1, oz), block, block, (at([(d2, o2)]), ctx))

    def pass_on(oz):
        for h in range(2):
            for o1 in range(1, dims[order[h][0]]):
                spread_second(h, oz, o1)

    for h in range(2):
        spread_first(h, 0)
    for h in range(2):
        spread_second(h, 0, 0)

    tiles = depth.shape[1]

    def flag(level, place):
        return jnp.where(depth[0, place] >= level, 1.0, 0.0).astype(F32)

    def of(level, who):
        return sum(jnp.where(who == t, flag(level, t), 0.0) for t in range(tiles))

    own2 = of(2, ctx)
    valid2 = sum(flag(2, t) for t in range(tiles))
    valid3 = sum(flag(3, t) for t in range(tiles))
    for o in range(1, contexts):
        slot = contexts - o - 1
        arrive(("hid", o), peer_h.at[slot])
        arrive(("cot", o), peer_g.at[slot])
    cols = [pl.ds(j * width, width) for j in range(chunks)]
    square = jnp.zeros((tile, 1), F32)
    for c in cols:
        live_h = hid[0, :, c].astype(F32) * own2
        live_g = cot[0, :, c].astype(F32) * own2
        for s in range(contexts - 1):
            flag_s = of(2, lax.rem(ctx + s + 1, contexts))
            live_h = live_h + peer_h[s, :, c].astype(F32) * flag_s
            live_g = live_g + peer_g[s, :, c].astype(F32) * flag_s
        hL[:, c] = live_h.astype(BF)
        DY[0:tile, c] = live_g.astype(BF)
        DY[tile : 2 * tile, c] = (live_g * valid3).astype(BF)
        square = square + jnp.sum(live_h * live_h, -1, keepdims=True)
    inv2 = lax.rsqrt(square * (1.0 / D) + 1e-06)
    for c in cols:
        R[0:tile, c] = (hL[:, c].astype(F32) * inv2 * gain[:, c]).astype(BF)

    for oz in range(1, Z):
        for h in range(2):
            arrive(("gz", h, oz), piece(h, [(0, -oz)]))
            spread_first(h, oz)
        for h in range(2):
            spread_second(h, oz, 0)
        pass_on(oz - 1)
    pass_on(Z - 1)

    group = D // Z

    def group_of(oz):
        return pl.ds(pl.multiple_of(lax.rem(zz + oz + Z, Z) * group, group), group)

    for oz in range(Z):
        for h in range(2):
            d1, d2 = order[h]
            for o1 in range(dims[d1]):
                for o2 in range(1, dims[d2]):
                    arrive(("g2", h, o2, o1, oz), piece(h, [(0, -oz), (d1, -o1), (d2, -o2)]))
        g = group_of(-oz)
        rows, grads = R[0:tile, g], DY[0:tile, g]
        part_a = nn(rows, WA[g, :])
        part_b = nn(jnp.concatenate([rows, grads], axis=0), WB[g, :])
        accA[...] = part_a if oz == 0 else accA[...] + part_a
        accB[...] = part_b if oz == 0 else accB[...] + part_b
        WAT[:, g] = WA[g, :].T
        WBT[:, g] = WB[g, :].T

    causal = lax.broadcasted_iota(jnp.int32, (tile, tile), 1) <= lax.broadcasted_iota(
        jnp.int32, (tile, tile), 0
    )
    scale = HD ** (-0.5)

    def attend(qk, value, valid):
        allowed = causal & (jnp.broadcast_to(valid, causal.shape) > 0.5)
        qk, value = qk.astype(BF), value.astype(BF)
        query, key = qk[:, 0:HD], qk[:, HD : 2 * HD]
        scores = jnp.where(allowed, nt(query, key) * scale, -1e30)
        expo = jnp.exp(scores - jnp.max(scores, -1, keepdims=True))
        prob = expo / jnp.sum(expo, -1, keepdims=True)
        probb = prob.astype(BF)
        attn = nn(probb, value).astype(BF)
        return query, key, value, prob, probb, attn

    def swap_out(name, term):
        e = EXCHANGES.index(name)
        for j in range(chunks):
            own_x[e, j] = term(cols[j]).astype(BF)
            for o in range(1, contexts):
                send((name, o, j), own_x.at[e, j], got_x.at[e, contexts - o - 1, j], ctx_peer(o))

    def swap_in(name, j):
        e = EXCHANGES.index(name)
        total = own_x[e, j].astype(F32)
        for o in range(1, contexts):
            slot = contexts - o - 1
            arrive((name, o, j), got_x.at[e, slot, j])
            total = total + got_x[e, slot, j].astype(F32)
        return total

    def backward(keep, dattn):
        query, key, value, prob, probb, attn = keep
        delta = jnp.sum(dattn.astype(F32) * attn.astype(F32), -1, keepdims=True)
        dscore = (prob * (nt(dattn, value) - delta) * scale).astype(BF)
        dq = nn(dscore, key).astype(BF)
        dk = nn(dscore.T, query).astype(BF)
        dv = nn(probb.T, dattn).astype(BF)
        return jnp.concatenate([dq, dk], axis=1), dv

    keep2 = attend(accA[...], accB[0:tile, 0:HD], valid2)
    swap_out("mix2", lambda c: nn(keep2[5], WBT[HD : 2 * HD, c]))
    grad_out3 = accB[tile : 2 * tile, HD : 2 * HD]
    dattn3 = (grad_out3 * valid3).astype(BF)
    square = jnp.zeros((tile, 1), F32)
    qk3 = jnp.zeros((tile, 2 * HD), F32)
    vo3 = jnp.zeros((2 * tile, 2 * HD), F32)
    for j, c in enumerate(cols):
        state = (hL[:, c].astype(F32) + swap_in("mix2", j)).astype(BF)
        h2[:, c] = state
        wide = state.astype(F32)
        square = square + jnp.sum(wide * wide, -1, keepdims=True)
        gained = (wide * gain[:, c]).astype(BF)
        qk3 = qk3 + nn(gained, WA[c, :])
        vo3 = vo3 + nn(jnp.concatenate([gained, state], axis=0), WB[c, :])
    inv3 = lax.rsqrt(square * (1.0 / D) + 1e-06)
    state_out = vo3[tile : 2 * tile, HD : 2 * HD]

    factor3 = inv3 * valid3
    keep3 = attend(qk3 * factor3, vo3[0:tile, 0:HD] * factor3, valid3)
    dqk3, dv3 = backward(keep3, dattn3)
    swap_out("dn3", lambda c: nn(dqk3, WAT[:, c]) + nn(dv3, WBT[0:HD, c]))
    swap_out("mix3", lambda c: nn(keep3[5], WBT[HD : 2 * HD, c]))
    for c in cols:
        R[tile : 2 * tile, c] = (h2[:, c].astype(F32) * inv3 * gain[:, c] * valid3).astype(BF)

    def norm_grad(name, state, inv, on, term):
        dot = jnp.zeros((tile, 1), F32)
        for j, c in enumerate(cols):
            u = swap_in(name, j) * gain[:, c]
            scaled[:, c] = u
            dot = dot + jnp.sum(u * state[:, c].astype(F32), -1, keepdims=True)
            term(c, u)
        return inv * on, inv * inv * inv * (dot * (1.0 / D)) * on

    def norm_apply(state, c, first, second):
        return scaled[:, c] * first - state[:, c].astype(F32) * second

    back = [jnp.zeros((tile, HD), F32)]

    def back_term(c, u):
        back[0] = back[0] + nn(u.astype(BF), WB[c, HD : 2 * HD])

    first, second = norm_grad("dn3", h2, inv3, valid3, back_term)
    dattn2 = (grad_out3 + back[0] * first - state_out * second).astype(BF)
    dqk2, dv2 = backward(keep2, dattn2)
    for c in cols:
        DY[0:tile, c] = (DY[0:tile, c].astype(F32) + norm_apply(h2, c, first, second)).astype(BF)

    left_a = jnp.concatenate([dqk2, dqk3], axis=0).T
    left_v = jnp.concatenate([dv2, dv3], axis=0).T
    left_o = jnp.concatenate([keep2[5], keep3[5]], axis=0).T
    plane = Y * X

    def cut(rows, block, z):
        for i in range(plane):
            G[z * plane + i, rows, :] = block[:, i * dloc : (i + 1) * dloc].astype(BF)

    got1, got2, sum1 = (R1a, R1b), (R2a, R2b), (T1a, T1b)

    def half_rows(h):
        return pl.ds(h * 2 * HD, 2 * HD)

    for oz in (*range(1, Z), 0):
        g = group_of(oz)
        z = lax.rem(zz + oz, Z)
        cut(pl.ds(0, 2 * HD), nn(left_a, R[:, g]), z)
        cut(pl.ds(2 * HD, HD), nn(left_v, R[:, g]), z)
        cut(pl.ds(3 * HD, HD), nn(left_o, DY[:, g]), z)
        for o2 in reversed(range(max(X, Y))):
            for h in range(2):
                e2, e1 = order[h]
                for o1 in range(1, dims[e1] if o2 < dims[e2] else 1):
                    send(
                        ("s1", h, o1, o2, oz),
                        G.at[at([(0, oz), (e1, o1), (e2, o2)]), half_rows(h), :],
                        got1[h].at[o1 - 1, o2, oz],
                        (at([(e1, o1)]), ctx),
                    )
    swap_out("dn2", lambda c: nn(dqk2, WAT[:, c]) + nn(dv2, WBT[0:HD, c]))

    not2 = 1.0 - own2
    for j, c in enumerate(cols):
        state = (h2[:, c].astype(F32) + swap_in("mix3", j)).astype(BF).astype(F32)
        hout[0, :, c] = (hid[0, :, c].astype(F32) * not2 + state * own2).astype(BF)

    def first_total(h, o2, oz):
        e2, e1 = order[h]
        total = G[at([(0, oz), (e2, o2)]), half_rows(h), :].astype(F32)
        for o1 in range(1, dims[e1]):
            arrive(("s1", h, o1, o2, oz), got1[h].at[o1 - 1, o2, oz])
            total = total + got1[h][o1 - 1, o2, oz].astype(F32)
        return total

    for oz in (*range(1, Z), 0):
        for h in range(2):
            e2, e1 = order[h]
            for o2 in range(1, dims[e2]):
                sum1[h][o2 - 1, oz] = first_total(h, o2, oz).astype(BF)
                send(
                    ("s2", h, o2, oz), sum1[h].at[o2 - 1, oz], got2[h].at[o2 - 1, oz],
                    (at([(e2, o2)]), ctx),
                )

    first, second = norm_grad("dn2", hL, inv2, 1.0, lambda c, u: None)
    for c in cols:
        grad = DY[0:tile, c].astype(F32) + norm_apply(hL, c, first, second)
        grad = grad.astype(BF).astype(F32)
        gout[0, :, c] = (cot[0, :, c].astype(F32) * not2 + grad * own2).astype(BF)

    def second_total(h, oz):
        total = first_total(h, 0, oz)
        for o2 in range(1, dims[order[h][0]]):
            arrive(("s2", h, o2, oz), got2[h].at[o2 - 1, oz])
            total = total + got2[h][o2 - 1, oz].astype(F32)
        return total

    for oz in range(1, Z):
        for h in range(2):
            T2[h, oz - 1] = second_total(h, oz).astype(BF)
            send(("s3", h, oz), T2.at[h, oz - 1], R3.at[h, oz - 1], (at([(0, oz)]), ctx))
    final = [second_total(h, 0) for h in range(2)]
    for h in range(2):
        for oz in range(1, Z):
            arrive(("s3", h, oz), R3.at[h, oz - 1])
            final[h] = final[h] + R3[h, oz - 1].astype(F32)
    gqkv[0] = final[0][0:HD].T
    gqkv[1] = final[0][HD : 2 * HD].T
    gqkv[2] = final[1][0:HD].T
    gwo[...] = final[1][HD : 2 * HD]

    for c in started:
        c.wait_send()


def write_out(parts, *refs):
    sources, targets, sems = refs[:4], refs[4:8], refs[8]
    copies = []
    for number, (i, part) in enumerate(parts):
        index = (0, part) if i < 2 else part
        copies.append(
            pltpu.make_async_copy(sources[i].at[index], targets[i].at[index], sems.at[number])
        )
    for c in copies:
        c.start()
    for c in copies:
        c.wait()


def on_device(hidden_in, cotangent, tile_depth, w_qkv, w_out, gain):
    contexts = lax.axis_size("context")
    n = lax.axis_size("dp")
    dims = grid_of(n)
    Z, Y, X = dims
    _, tile, D = hidden_in.shape
    dloc = w_qkv.shape[1]
    chunks = 4
    width = D // chunks
    keys = copy_keys(dims, contexts, chunks)
    others = max(1, contexts - 1)
    vmem = pl.BlockSpec(memory_space=pltpu.VMEM)

    def block(*lead):
        return pltpu.VMEM((*[max(1, v) for v in lead], 2 * HD, dloc), BF)

    results = pl.pallas_call(
        functools.partial(kernel, dims, contexts, chunks, keys),
        out_shape=(
            jax.ShapeDtypeStruct(hidden_in.shape, BF),
            jax.ShapeDtypeStruct(cotangent.shape, BF),
            jax.ShapeDtypeStruct(w_qkv.shape, F32),
            jax.ShapeDtypeStruct(w_out.shape, F32),
        ),
        in_specs=[pl.BlockSpec(memory_space=pltpu.SMEM)] + [vmem] * 5,
        out_specs=(vmem,) * 4,
        scratch_shapes=[
            pltpu.VMEM((D, 2 * HD), BF),
            pltpu.VMEM((D, 2 * HD), BF),
            pltpu.VMEM((2 * HD, D), BF),
            pltpu.VMEM((2 * HD, D), BF),
            pltpu.VMEM((tile, 2 * HD), F32),
            pltpu.VMEM((2 * tile, 2 * HD), F32),
            pltpu.VMEM((others, tile, D), BF),
            pltpu.VMEM((others, tile, D), BF),
            pltpu.VMEM((tile, D), BF),
            pltpu.VMEM((tile, D), BF),
            pltpu.VMEM((2 * tile, D), BF),
            pltpu.VMEM((2 * tile, D), BF),
            pltpu.VMEM((tile, D), F32),
            pltpu.VMEM((len(EXCHANGES), chunks, tile, width), BF),
            pltpu.VMEM((len(EXCHANGES), others, chunks, tile, width), BF),
            pltpu.VMEM((n, 4 * HD, dloc), BF),
            block(Y - 1, X, Z),
            block(X - 1, Y, Z),
            block(X - 1, Z),
            block(Y - 1, Z),
            block(2, Z - 1),
            block(X - 1, Z),
            block(Y - 1, Z),
            block(2, Z - 1),
            pltpu.SemaphoreType.DMA((len(keys),)),
            pltpu.SemaphoreType.DMA((len(keys),)),
        ],
        compiler_params=pltpu.CompilerParams(
            collective_id=0, has_side_effects=True, vmem_limit_bytes=60 * 1024 * 1024
        ),
        cost_estimate=pl.CostEstimate(
            flops=16 * tile * D * 3 * HD, bytes_accessed=8 * tile * D, transcendentals=tile * tile
        ),
        name="recursion_sublayer",
    )(tile_depth, hidden_in, cotangent, w_qkv, w_out, gain[None, :])
    parts = [(i, slice(p * tile // 4, (p + 1) * tile // 4)) for i in (0, 1) for p in range(4)]
    parts += [(2, t) for t in range(3)] + [(3, slice(None))]
    anywhere = pl.BlockSpec(memory_space=pl.ANY)
    return pl.pallas_call(
        functools.partial(write_out, parts),
        out_shape=tuple(jax.ShapeDtypeStruct(r.shape, r.dtype) for r in results),
        in_specs=[anywhere] * 4,
        out_specs=(anywhere,) * 4,
        scratch_shapes=[pltpu.SemaphoreType.DMA((len(parts),))],
        name="write_outputs",
    )(*results)


def solution(mesh):
    in_specs = (
        P("dp", "context", None),
        P("dp", "context", None),
        P("dp", None),
        P(None, "dp", "context"),
        P("context", "dp"),
        P(),
    )
    out_specs = (
        P("dp", "context", None),
        P("dp", "context", None),
        P(None, "dp", "context"),
        P("context", "dp"),
    )
    return jax.shard_map(
        on_device, mesh=mesh, in_specs=in_specs, out_specs=out_specs, check_vma=False
    )
```

```python
import functools

import jax
import jax.numpy as jnp
from jax import lax
from jax.experimental import pallas as pl
from jax.experimental.pallas import tpu as pltpu
from jax.sharding import PartitionSpec as P

HD = 128
MESH = pl.DeviceIdType.MESH
BF = jnp.bfloat16
F32 = jnp.float32
EXCHANGES = ("mix2", "mix3", "dn3", "dn2")


def grid_of(n):
    if n == 64:
        return (16, 4, 1)
    if n % 4 == 0:
        return (n // 4, 2, 2)
    return (n, 1, 1)


def copy_keys(dims, contexts, chunks):
    Z, Y, X = dims
    first = (X, Y)
    second = (Y, X)
    keys = [(name, o) for o in range(1, contexts) for name in ("hid", "cot")]
    keys += [(n, o, j) for n in EXCHANGES for o in range(1, contexts) for j in range(chunks)]
    for h in range(2):
        keys += [("gz", h, oz) for oz in range(1, Z)]
        keys += [("g1", h, o1, oz) for o1 in range(1, first[h]) for oz in range(Z)]
        keys += [
            ("g2", h, o2, o1, oz)
            for o2 in range(1, second[h])
            for o1 in range(first[h])
            for oz in range(Z)
        ]
    for h in range(2):
        keys += [
            ("s1", h, o1, o2, oz)
            for o1 in range(1, second[h])
            for o2 in range(first[h])
            for oz in range(Z)
        ]
        keys += [("s2", h, o2, oz) for o2 in range(1, first[h]) for oz in range(Z)]
        keys += [("s3", h, oz) for oz in range(1, Z)]
    return {key: number for number, key in enumerate(keys)}


def nn(a, b):
    return jnp.dot(a, b, preferred_element_type=F32)


def nt(a, b):
    return lax.dot_general(a, b, (((1,), (1,)), ((), ())), preferred_element_type=F32)


def kernel(
    dims, contexts, chunks, keys,
    depth, hid, cot, wq, wo, gain,
    hout, gout, gqkv, gwo,
    WA, WB, WAT, WBT, accA, accB, peer_h, peer_g, hL, h2, R, DY, scaled, own_x, got_x,
    G, R1a, R1b, R2a, R2b, R3, T1a, T1b, T2, send_sem, recv_sem,
):
    Z, Y, X = dims
    dp = lax.axis_index("dp")
    ctx = lax.axis_index("context")
    zz, yy, xx = dp // (Y * X), lax.rem(dp // X, Y), lax.rem(dp, X)
    tile, D = hid.shape[1], hid.shape[2]
    dloc = wq.shape[1]
    width = D // chunks
    me = (zz, yy, xx)
    order = ((2, 1), (1, 2))

    def spot(**moves):
        place = list(me)
        for name, off in moves.items():
            axis = int(name[1])
            if not (isinstance(off, int) and off == 0):
                place[axis] = lax.rem(me[axis] + off + dims[axis], dims[axis])
        return (place[0] * Y + place[1]) * X + place[2]

    def at(axes):
        return spot(**{"a%d" % axis: off for axis, off in axes})

    def number_of(key):
        low = 0 if (*key[:-1], 0) in keys else 1
        return keys[(*key[:-1], low)] + (key[-1] - low)

    def copy(number, src, dst, peer):
        return pltpu.make_async_remote_copy(
            src_ref=src, dst_ref=dst, send_sem=send_sem.at[number], recv_sem=recv_sem.at[number],
            device_id=peer, device_id_type=MESH,
        )

    def send(key, src, dst, peer):
        copy(number_of(key), src, dst, peer).start()

    def loop(low, high, body):
        def step(i, carry):
            body(i)
            return carry

        if high > low:
            lax.fori_loop(low, high, step, 0)

    def arrive(key, dst):
        copy(number_of(key), dst, dst, (dp, ctx)).wait_recv()

    def ctx_peer(o):
        return (dp, lax.rem(ctx + o, contexts))

    barrier = pltpu.get_barrier_semaphore()
    peers = [(at([(axis, o)]), ctx) for axis in range(3) for o in range(1, dims[axis])]
    peers += [ctx_peer(o) for o in range(1, contexts)]
    for peer in peers:
        pl.semaphore_signal(barrier, inc=1, device_id=peer, device_id_type=MESH)

    mine = pl.ds(pl.multiple_of(dp * dloc, dloc), dloc)
    WA[mine, 0:HD] = wq[0]
    WA[mine, HD : 2 * HD] = wq[1]
    WB[mine, 0:HD] = wq[2]
    WB[mine, HD : 2 * HD] = wo[...].T
    pl.semaphore_wait(barrier, len(peers))

    halves = (WA, WB)

    def piece(h, axes):
        p = at(axes)
        return halves[h].at[pl.ds(pl.multiple_of(p * dloc, dloc), dloc), :]

    for h in range(2):
        for oz in range(1, Z):
            block = piece(h, [])
            send(("gz", h, oz), block, block, (at([(0, oz)]), ctx))
    for o in range(1, contexts):
        slot = contexts - o - 1
        send(("hid", o), hid.at[0], peer_h.at[slot], ctx_peer(o))
        send(("cot", o), cot.at[0], peer_g.at[slot], ctx_peer(o))

    def spread_first(h, oz):
        d1 = order[h][0]
        block = piece(h, [(0, -oz)])
        for o1 in range(1, dims[d1]):
            send(("g1", h, o1, oz), block, block, (at([(d1, o1)]), ctx))

    def spread_second(h, oz, o1):
        d1, d2 = order[h]
        block = piece(h, [(0, -oz), (d1, -o1)])
        if o1:
            arrive(("g1", h, o1, oz), block)
        for o2 in range(1, dims[d2]):
            send(("g2", h, o2, o1, oz), block, block, (at([(d2, o2)]), ctx))

    def pass_on(oz):
        for h in range(2):
            for o1 in range(1, dims[order[h][0]]):
                spread_second(h, oz, o1)

    for h in range(2):
        spread_first(h, 0)
    for h in range(2):
        spread_second(h, 0, 0)

    tiles = depth.shape[1]

    def flag(level, place):
        return jnp.where(depth[0, place] >= level, 1.0, 0.0).astype(F32)

    def of(level, who):
        return sum(jnp.where(who == t, flag(level, t), 0.0) for t in range(tiles))

    own2 = of(2, ctx)
    valid2 = sum(flag(2, t) for t in range(tiles))
    valid3 = sum(flag(3, t) for t in range(tiles))
    for o in range(1, contexts):
        slot = contexts - o - 1
        arrive(("hid", o), peer_h.at[slot])
        arrive(("cot", o), peer_g.at[slot])
    no_rows = jnp.zeros((tile, 1), F32)

    def col(j):
        return pl.ds(pl.multiple_of(j * width, HD), width)

    def take_live(j, square):
        c = col(j)
        live_h = hid[0, :, c].astype(F32) * own2
        live_g = cot[0, :, c].astype(F32) * own2
        for s in range(contexts - 1):
            flag_s = of(2, lax.rem(ctx + s + 1, contexts))
            live_h = live_h + peer_h[s, :, c].astype(F32) * flag_s
            live_g = live_g + peer_g[s, :, c].astype(F32) * flag_s
        hL[:, c] = live_h.astype(BF)
        DY[0:tile, c] = live_g.astype(BF)
        DY[tile : 2 * tile, c] = (live_g * valid3).astype(BF)
        return square + jnp.sum(live_h * live_h, -1, keepdims=True)

    square = lax.fori_loop(0, chunks, take_live, no_rows)
    inv2 = lax.rsqrt(square * (1.0 / D) + 1e-06)

    @functools.partial(loop, 0, chunks)
    def _(j):
        c = col(j)
        R[0:tile, c] = (hL[:, c].astype(F32) * inv2 * gain[:, c]).astype(BF)

    def from_z(oz):
        for h in range(2):
            arrive(("gz", h, oz), piece(h, [(0, -oz)]))
            spread_first(h, oz)
        for h in range(2):
            spread_second(h, oz, 0)
        pass_on(oz - 1)

    loop(1, Z, from_z)
    pass_on(Z - 1)

    group = D // Z

    def group_of(oz):
        return pl.ds(pl.multiple_of(lax.rem(zz + oz + Z, Z) * group, group), group)

    accA[...] = jnp.zeros_like(accA)
    accB[...] = jnp.zeros_like(accB)

    @functools.partial(loop, 0, Z)
    def _(oz):
        for h in range(2):
            d1, d2 = order[h]
            for o1 in range(dims[d1]):
                for o2 in range(1, dims[d2]):
                    arrive(("g2", h, o2, o1, oz), piece(h, [(0, -oz), (d1, -o1), (d2, -o2)]))
        g = group_of(-oz)
        rows, grads = R[0:tile, g], DY[0:tile, g]
        accA[...] += nn(rows, WA[g, :])
        accB[...] += nn(jnp.concatenate([rows, grads], axis=0), WB[g, :])
        WAT[:, g] = WA[g, :].T
        WBT[:, g] = WB[g, :].T

    causal = lax.broadcasted_iota(jnp.int32, (tile, tile), 1) <= lax.broadcasted_iota(
        jnp.int32, (tile, tile), 0
    )
    scale = HD ** (-0.5)

    def attend(qk, value, valid):
        allowed = causal & (jnp.broadcast_to(valid, causal.shape) > 0.5)
        qk, value = qk.astype(BF), value.astype(BF)
        query, key = qk[:, 0:HD], qk[:, HD : 2 * HD]
        scores = jnp.where(allowed, nt(query, key) * scale, -1e30)
        expo = jnp.exp(scores - jnp.max(scores, -1, keepdims=True))
        prob = expo / jnp.sum(expo, -1, keepdims=True)
        probb = prob.astype(BF)
        attn = nn(probb, value).astype(BF)
        return query, key, value, prob, probb, attn

    def swap_out(name, term):
        e = EXCHANGES.index(name)

        @functools.partial(loop, 0, chunks)
        def _(j):
            own_x[e, j] = term(col(j)).astype(BF)
            for o in range(1, contexts):
                send((name, o, j), own_x.at[e, j], got_x.at[e, contexts - o - 1, j], ctx_peer(o))

    def swap_in(name, j):
        e = EXCHANGES.index(name)
        total = own_x[e, j].astype(F32)
        for o in range(1, contexts):
            slot = contexts - o - 1
            arrive((name, o, j), got_x.at[e, slot, j])
            total = total + got_x[e, slot, j].astype(F32)
        return total

    def backward(keep, dattn):
        query, key, value, prob, probb, attn = keep
        delta = jnp.sum(dattn.astype(F32) * attn.astype(F32), -1, keepdims=True)
        dscore = (prob * (nt(dattn, value) - delta) * scale).astype(BF)
        dq = nn(dscore, key).astype(BF)
        dk = nn(dscore.T, query).astype(BF)
        dv = nn(probb.T, dattn).astype(BF)
        return jnp.concatenate([dq, dk], axis=1), dv

    keep2 = attend(accA[...], accB[0:tile, 0:HD], valid2)
    swap_out("mix2", lambda c: nn(keep2[5], WBT[HD : 2 * HD, c]))
    grad_out3 = accB[tile : 2 * tile, HD : 2 * HD]
    dattn3 = (grad_out3 * valid3).astype(BF)

    def take_mix2(j, carry):
        square, qk, vo = carry
        c = col(j)
        state = (hL[:, c].astype(F32) + swap_in("mix2", j)).astype(BF)
        h2[:, c] = state
        wide = state.astype(F32)
        gained = (wide * gain[:, c]).astype(BF)
        return (
            square + jnp.sum(wide * wide, -1, keepdims=True),
            qk + nn(gained, WA[c, :]),
            vo + nn(jnp.concatenate([gained, state], axis=0), WB[c, :]),
        )

    square, qk3, vo3 = lax.fori_loop(
        0, chunks, take_mix2,
        (no_rows, jnp.zeros((tile, 2 * HD), F32), jnp.zeros((2 * tile, 2 * HD), F32)),
    )
    inv3 = lax.rsqrt(square * (1.0 / D) + 1e-06)
    state_out = vo3[tile : 2 * tile, HD : 2 * HD]

    factor3 = inv3 * valid3
    keep3 = attend(qk3 * factor3, vo3[0:tile, 0:HD] * factor3, valid3)
    dqk3, dv3 = backward(keep3, dattn3)
    swap_out("dn3", lambda c: nn(dqk3, WAT[:, c]) + nn(dv3, WBT[0:HD, c]))
    swap_out("mix3", lambda c: nn(keep3[5], WBT[HD : 2 * HD, c]))

    @functools.partial(loop, 0, chunks)
    def _(j):
        c = col(j)
        R[tile : 2 * tile, c] = (h2[:, c].astype(F32) * inv3 * gain[:, c] * valid3).astype(BF)

    def norm_grad(name, state, inv, on, start, term):
        def step(j, carry):
            dot, back = carry
            c = col(j)
            u = swap_in(name, j) * gain[:, c]
            scaled[:, c] = u
            return dot + jnp.sum(u * state[:, c].astype(F32), -1, keepdims=True), term(c, u, back)

        dot, back = lax.fori_loop(0, chunks, step, (no_rows, start))
        return inv * on, inv * inv * inv * (dot * (1.0 / D)) * on, back

    def norm_apply(state, c, first, second):
        return scaled[:, c] * first - state[:, c].astype(F32) * second

    first3, second3, back = norm_grad(
        "dn3", h2, inv3, valid3, jnp.zeros((tile, HD), F32),
        lambda c, u, back: back + nn(u.astype(BF), WB[c, HD : 2 * HD]),
    )
    dattn2 = (grad_out3 + back * first3 - state_out * second3).astype(BF)
    dqk2, dv2 = backward(keep2, dattn2)

    @functools.partial(loop, 0, chunks)
    def _(j):
        c = col(j)
        DY[0:tile, c] = (DY[0:tile, c].astype(F32) + norm_apply(h2, c, first3, second3)).astype(BF)

    left_a = jnp.concatenate([dqk2, dqk3], axis=0).T
    left_v = jnp.concatenate([dv2, dv3], axis=0).T
    left_o = jnp.concatenate([keep2[5], keep3[5]], axis=0).T
    plane = Y * X

    def cut(rows, block, z):
        for i in range(plane):
            G[z * plane + i, rows, :] = block[:, i * dloc : (i + 1) * dloc].astype(BF)

    got1, got2, sum1 = (R1a, R1b), (R2a, R2b), (T1a, T1b)

    def half_rows(h):
        return pl.ds(h * 2 * HD, 2 * HD)

    @functools.partial(loop, 0, Z)
    def _(i):
        oz = lax.rem(i + 1, Z)
        g = group_of(oz)
        z = lax.rem(zz + oz, Z)
        cut(pl.ds(0, 2 * HD), nn(left_a, R[:, g]), z)
        cut(pl.ds(2 * HD, HD), nn(left_v, R[:, g]), z)
        cut(pl.ds(3 * HD, HD), nn(left_o, DY[:, g]), z)
        for o2 in reversed(range(max(X, Y))):
            for h in range(2):
                e2, e1 = order[h]
                for o1 in range(1, dims[e1] if o2 < dims[e2] else 1):
                    send(
                        ("s1", h, o1, o2, oz),
                        G.at[at([(0, oz), (e1, o1), (e2, o2)]), half_rows(h), :],
                        got1[h].at[o1 - 1, o2, oz],
                        (at([(e1, o1)]), ctx),
                    )
    swap_out("dn2", lambda c: nn(dqk2, WAT[:, c]) + nn(dv2, WBT[0:HD, c]))

    not2 = 1.0 - own2

    @functools.partial(loop, 0, chunks)
    def _(j):
        c = col(j)
        state = (h2[:, c].astype(F32) + swap_in("mix3", j)).astype(BF).astype(F32)
        hout[0, :, c] = (hid[0, :, c].astype(F32) * not2 + state * own2).astype(BF)

    def first_total(h, o2, oz):
        e2, e1 = order[h]
        total = G[at([(0, oz), (e2, o2)]), half_rows(h), :].astype(F32)
        for o1 in range(1, dims[e1]):
            arrive(("s1", h, o1, o2, oz), got1[h].at[o1 - 1, o2, oz])
            total = total + got1[h][o1 - 1, o2, oz].astype(F32)
        return total

    @functools.partial(loop, 0, Z)
    def _(i):
        oz = lax.rem(i + 1, Z)
        for h in range(2):
            e2, e1 = order[h]
            for o2 in range(1, dims[e2]):
                sum1[h][o2 - 1, oz] = first_total(h, o2, oz).astype(BF)
                send(
                    ("s2", h, o2, oz), sum1[h].at[o2 - 1, oz], got2[h].at[o2 - 1, oz],
                    (at([(e2, o2)]), ctx),
                )

    first2, second2, _ = norm_grad("dn2", hL, inv2, 1.0, 0, lambda c, u, back: back)

    @functools.partial(loop, 0, chunks)
    def _(j):
        c = col(j)
        grad = DY[0:tile, c].astype(F32) + norm_apply(hL, c, first2, second2)
        grad = grad.astype(BF).astype(F32)
        gout[0, :, c] = (cot[0, :, c].astype(F32) * not2 + grad * own2).astype(BF)

    def second_total(h, oz):
        total = first_total(h, 0, oz)
        for o2 in range(1, dims[order[h][0]]):
            arrive(("s2", h, o2, oz), got2[h].at[o2 - 1, oz])
            total = total + got2[h][o2 - 1, oz].astype(F32)
        return total

    @functools.partial(loop, 1, Z)
    def _(oz):
        for h in range(2):
            T2[h, oz - 1] = second_total(h, oz).astype(BF)
            send(("s3", h, oz), T2.at[h, oz - 1], R3.at[h, oz - 1], (at([(0, oz)]), ctx))
    final = [second_total(h, 0) for h in range(2)]
    for h in range(2):
        for oz in range(1, Z):
            arrive(("s3", h, oz), R3.at[h, oz - 1])
            final[h] = final[h] + R3[h, oz - 1].astype(F32)
    gqkv[0] = final[0][0:HD].T
    gqkv[1] = final[0][HD : 2 * HD].T
    gqkv[2] = final[1][0:HD].T
    gwo[...] = final[1][HD : 2 * HD]

    def sent(kinds, block):
        numbers = [number for key, number in keys.items() if key[0] in kinds]
        if numbers:
            loop(min(numbers), max(numbers) + 1, lambda k: copy(k, block, block, (dp, ctx)).wait_send())

    sent(("hid", "cot"), hid.at[0])
    sent(EXCHANGES, own_x.at[0, 0])
    sent(("gz", "g1", "g2"), piece(0, []))
    sent(("s1", "s2", "s3"), T2.at[0, 0])


def write_out(*refs):
    sources, targets, sems = refs[:4], refs[4:8], refs[8]
    copies = [pltpu.make_async_copy(sources[i], targets[i], sems.at[i]) for i in range(4)]
    for c in copies:
        c.start()
    for c in copies:
        c.wait()


def on_device(hidden_in, cotangent, tile_depth, w_qkv, w_out, gain):
    contexts = lax.axis_size("context")
    n = lax.axis_size("dp")
    dims = grid_of(n)
    Z, Y, X = dims
    _, tile, D = hidden_in.shape
    dloc = w_qkv.shape[1]
    chunks = 4
    width = D // chunks
    keys = copy_keys(dims, contexts, chunks)
    others = max(1, contexts - 1)
    vmem = pl.BlockSpec(memory_space=pltpu.VMEM)

    def block(*lead):
        return pltpu.VMEM((*[max(1, v) for v in lead], 2 * HD, dloc), BF)

    results = pl.pallas_call(
        functools.partial(kernel, dims, contexts, chunks, keys),
        out_shape=(
            jax.ShapeDtypeStruct(hidden_in.shape, BF),
            jax.ShapeDtypeStruct(cotangent.shape, BF),
            jax.ShapeDtypeStruct(w_qkv.shape, F32),
            jax.ShapeDtypeStruct(w_out.shape, F32),
        ),
        in_specs=[pl.BlockSpec(memory_space=pltpu.SMEM)] + [vmem] * 5,
        out_specs=(vmem,) * 4,
        scratch_shapes=[
            pltpu.VMEM((D, 2 * HD), BF),
            pltpu.VMEM((D, 2 * HD), BF),
            pltpu.VMEM((2 * HD, D), BF),
            pltpu.VMEM((2 * HD, D), BF),
            pltpu.VMEM((tile, 2 * HD), F32),
            pltpu.VMEM((2 * tile, 2 * HD), F32),
            pltpu.VMEM((others, tile, D), BF),
            pltpu.VMEM((others, tile, D), BF),
            pltpu.VMEM((tile, D), BF),
            pltpu.VMEM((tile, D), BF),
            pltpu.VMEM((2 * tile, D), BF),
            pltpu.VMEM((2 * tile, D), BF),
            pltpu.VMEM((tile, D), F32),
            pltpu.VMEM((len(EXCHANGES), chunks, tile, width), BF),
            pltpu.VMEM((len(EXCHANGES), others, chunks, tile, width), BF),
            pltpu.VMEM((n, 4 * HD, dloc), BF),
            block(Y - 1, X, Z),
            block(X - 1, Y, Z),
            block(X - 1, Z),
            block(Y - 1, Z),
            block(2, Z - 1),
            block(X - 1, Z),
            block(Y - 1, Z),
            block(2, Z - 1),
            pltpu.SemaphoreType.DMA((len(keys),)),
            pltpu.SemaphoreType.DMA((len(keys),)),
        ],
        compiler_params=pltpu.CompilerParams(
            collective_id=0, has_side_effects=True, vmem_limit_bytes=60 * 1024 * 1024
        ),
        cost_estimate=pl.CostEstimate(
            flops=16 * tile * D * 3 * HD, bytes_accessed=8 * tile * D, transcendentals=tile * tile
        ),
        name="recursion_sublayer",
    )(tile_depth, hidden_in, cotangent, w_qkv, w_out, gain[None, :])
    return pl.pallas_call(
        write_out,
        out_shape=tuple(jax.ShapeDtypeStruct(r.shape, r.dtype) for r in results),
        in_specs=[vmem] * 4,
        out_specs=(pl.BlockSpec(memory_space=pl.ANY),) * 4,
        scratch_shapes=[pltpu.SemaphoreType.DMA((4,))],
        name="write_outputs",
    )(*results)


def solution(mesh):
    in_specs = (
        P("dp", "context", None),
        P("dp", "context", None),
        P("dp", None),
        P(None, "dp", "context"),
        P("context", "dp"),
        P(),
    )
    out_specs = (
        P("dp", "context", None),
        P("dp", "context", None),
        P(None, "dp", "context"),
        P("context", "dp"),
    )
    return jax.shard_map(
        on_device, mesh=mesh, in_specs=in_specs, out_specs=out_specs, check_vma=False
    )
```

```python
import functools

import jax
import jax.numpy as jnp
from jax import lax
from jax.experimental import pallas as pl
from jax.experimental.pallas import tpu as pltpu
from jax.sharding import PartitionSpec as P

HD = 128
MESH = pl.DeviceIdType.MESH
BF = jnp.bfloat16
F32 = jnp.float32
EXCHANGES = ("mix2", "mix3", "dn3", "dn2")


def grid_of(n):
    if n == 64:
        return (16, 4, 1)
    if n % 4 == 0:
        return (n // 4, 2, 2)
    return (n, 1, 1)


def copy_keys(dims, contexts, chunks):
    Z, Y, X = dims
    first = (X, Y)
    second = (Y, X)
    keys = [(name, o) for o in range(1, contexts) for name in ("hid", "cot")]
    keys += [(n, o, j) for n in EXCHANGES for o in range(1, contexts) for j in range(chunks)]
    for h in range(2):
        keys += [("gz", h, oz) for oz in range(1, Z)]
        keys += [(way, h, step) for way in ("up", "down") for step in range(Z - 1)]
        keys += [("g1", h, o1, oz) for o1 in range(1, first[h]) for oz in range(Z)]
        keys += [
            ("g2", h, o2, o1, oz)
            for o2 in range(1, second[h])
            for o1 in range(first[h])
            for oz in range(Z)
        ]
    for h in range(2):
        keys += [
            ("s1", h, o1, o2, oz)
            for o1 in range(1, second[h])
            for o2 in range(first[h])
            for oz in range(Z)
        ]
        keys += [("s2", h, o2, oz) for o2 in range(1, first[h]) for oz in range(Z)]
        keys += [("s3", h, oz) for oz in range(1, Z)]
    return {key: number for number, key in enumerate(keys)}


def nn(a, b):
    return jnp.dot(a, b, preferred_element_type=F32)


def nt(a, b):
    return lax.dot_general(a, b, (((1,), (1,)), ((), ())), preferred_element_type=F32)


def kernel(
    dims, contexts, chunks, keys,
    depth, hid, cot, wq, wo, gain,
    hout, gout, gqkv, gwo,
    WA, WB, WAT, WBT, accA, accB, peer_h, peer_g, hL, h2, R, DY, scaled, own_x, got_x,
    G, R1a, R1b, R2a, R2b, R3, T1a, T1b, T2, send_sem, recv_sem,
):
    Z, Y, X = dims
    dp = lax.axis_index("dp")
    ctx = lax.axis_index("context")
    zz, yy, xx = dp // (Y * X), lax.rem(dp // X, Y), lax.rem(dp, X)
    tile, D = hid.shape[1], hid.shape[2]
    dloc = wq.shape[1]
    width = D // chunks
    me = (zz, yy, xx)
    order = ((2, 1), (1, 2))

    def spot(**moves):
        place = list(me)
        for name, off in moves.items():
            axis = int(name[1])
            if not (isinstance(off, int) and off == 0):
                place[axis] = lax.rem(me[axis] + off + dims[axis], dims[axis])
        return (place[0] * Y + place[1]) * X + place[2]

    def at(axes):
        return spot(**{"a%d" % axis: off for axis, off in axes})

    def number_of(key):
        low = 0 if (*key[:-1], 0) in keys else 1
        return keys[(*key[:-1], low)] + (key[-1] - low)

    def copy(number, src, dst, peer, leaving=None):
        leaving = number if leaving is None else leaving
        return pltpu.make_async_remote_copy(
            src_ref=src, dst_ref=dst, send_sem=send_sem.at[leaving], recv_sem=recv_sem.at[number],
            device_id=peer, device_id_type=MESH,
        )

    def send(key, src, dst, peer, leaving=None):
        leaving = None if leaving is None else number_of(leaving)
        copy(number_of(key), src, dst, peer, leaving).start()

    def loop(low, high, body):
        def step(i, carry):
            body(i)
            return carry

        if high > low:
            lax.fori_loop(low, high, step, 0)

    def arrive(key, dst):
        copy(number_of(key), dst, dst, (dp, ctx)).wait_recv()

    def ctx_peer(o):
        return (dp, lax.rem(ctx + o, contexts))

    barrier = pltpu.get_barrier_semaphore()
    peers = [(at([(axis, o)]), ctx) for axis in range(3) for o in range(1, dims[axis])]
    peers += [ctx_peer(o) for o in range(1, contexts)]
    for peer in peers:
        pl.semaphore_signal(barrier, inc=1, device_id=peer, device_id_type=MESH)

    mine = pl.ds(pl.multiple_of(dp * dloc, dloc), dloc)
    WA[mine, 0:HD] = wq[0]
    WA[mine, HD : 2 * HD] = wq[1]
    WB[mine, 0:HD] = wq[2]
    WB[mine, HD : 2 * HD] = wo[...].T
    pl.semaphore_wait(barrier, len(peers))

    halves = (WA, WB)

    def piece(h, axes):
        p = at(axes)
        return halves[h].at[pl.ds(pl.multiple_of(p * dloc, dloc), dloc), :]

    def line_up(h, step):
        @pl.when((zz >= step) & (zz < Z - 1))
        def _():
            block = piece(h, [(0, -step)])
            send(("gz", h, step + 1), block, block, (at([(0, 1)]), ctx), ("up", h, step))

    def line_down(h, step):
        @pl.when((zz + step <= Z - 1) & (zz > 0))
        def _():
            block = piece(h, [(0, step)])
            send(("gz", h, Z - 1 - step), block, block, (at([(0, -1)]), ctx), ("down", h, step))

    def spread_first(h, oz):
        d1 = order[h][0]
        block = piece(h, [(0, -oz)])
        for o1 in range(1, dims[d1]):
            send(("g1", h, o1, oz), block, block, (at([(d1, o1)]), ctx))

    def spread_second(h, oz, o1):
        d1, d2 = order[h]
        block = piece(h, [(0, -oz), (d1, -o1)])
        if o1:
            arrive(("g1", h, o1, oz), block)
        for o2 in range(1, dims[d2]):
            send(("g2", h, o2, o1, oz), block, block, (at([(d2, o2)]), ctx))

    def pass_on(oz):
        for h in range(2):
            for o1 in range(1, dims[order[h][0]]):
                spread_second(h, oz, o1)

    for h in range(2):
        spread_first(h, 0)
        if Z > 1:
            line_up(h, 0)
            line_down(h, 0)
    for h in range(2):
        spread_second(h, 0, 0)
    for o in range(1, contexts):
        slot = contexts - o - 1
        send(("hid", o), hid.at[0], peer_h.at[slot], ctx_peer(o))
        send(("cot", o), cot.at[0], peer_g.at[slot], ctx_peer(o))

    tiles = depth.shape[1]

    def flag(level, place):
        return jnp.where(depth[0, place] >= level, 1.0, 0.0).astype(F32)

    def of(level, who):
        return sum(jnp.where(who == t, flag(level, t), 0.0) for t in range(tiles))

    own2 = of(2, ctx)
    valid2 = sum(flag(2, t) for t in range(tiles))
    valid3 = sum(flag(3, t) for t in range(tiles))
    for o in range(1, contexts):
        slot = contexts - o - 1
        arrive(("hid", o), peer_h.at[slot])
        arrive(("cot", o), peer_g.at[slot])
    no_rows = jnp.zeros((tile, 1), F32)

    def col(j):
        return pl.ds(pl.multiple_of(j * width, HD), width)

    def take_live(j, square):
        c = col(j)
        live_h = hid[0, :, c].astype(F32) * own2
        live_g = cot[0, :, c].astype(F32) * own2
        for s in range(contexts - 1):
            flag_s = of(2, lax.rem(ctx + s + 1, contexts))
            live_h = live_h + peer_h[s, :, c].astype(F32) * flag_s
            live_g = live_g + peer_g[s, :, c].astype(F32) * flag_s
        hL[:, c] = live_h.astype(BF)
        DY[0:tile, c] = live_g.astype(BF)
        DY[tile : 2 * tile, c] = (live_g * valid3).astype(BF)
        return square + jnp.sum(live_h * live_h, -1, keepdims=True)

    square = lax.fori_loop(0, chunks, take_live, no_rows)
    inv2 = lax.rsqrt(square * (1.0 / D) + 1e-06)

    @functools.partial(loop, 0, chunks)
    def _(j):
        c = col(j)
        R[0:tile, c] = (hL[:, c].astype(F32) * inv2 * gain[:, c]).astype(BF)

    def from_z(oz, step, line):
        for h in range(2):
            arrive(("gz", h, oz), piece(h, [(0, -oz)]))
            spread_first(h, oz)

            @pl.when(step < Z - 1)
            def _(h=h):
                line(h, step)

        for h in range(2):
            spread_second(h, oz, 0)

    def both_ways(step, act):
        @pl.when(zz >= step)
        def _():
            act(step, line_up)

        @pl.when(zz + step <= Z - 1)
        def _():
            act(Z - step, line_down)

    pass_on(0)

    @functools.partial(loop, 1, Z)
    def _(step):
        both_ways(step, lambda oz, line: from_z(oz, step, line))
        both_ways(step, lambda oz, line: pass_on(oz))

    group = D // Z

    def group_of(oz):
        return pl.ds(pl.multiple_of(lax.rem(zz + oz + Z, Z) * group, group), group)

    accA[...] = jnp.zeros_like(accA)
    accB[...] = jnp.zeros_like(accB)

    def project(oz):
        for h in range(2):
            d1, d2 = order[h]
            for o1 in range(dims[d1]):
                for o2 in range(1, dims[d2]):
                    arrive(("g2", h, o2, o1, oz), piece(h, [(0, -oz), (d1, -o1), (d2, -o2)]))
        g = group_of(-oz)
        rows, grads = R[0:tile, g], DY[0:tile, g]
        accA[...] += nn(rows, WA[g, :])
        accB[...] += nn(jnp.concatenate([rows, grads], axis=0), WB[g, :])
        WAT[:, g] = WA[g, :].T
        WBT[:, g] = WB[g, :].T

    project(0)

    @functools.partial(loop, 1, Z)
    def _(step):
        both_ways(step, lambda oz, line: project(oz))

    causal = lax.broadcasted_iota(jnp.int32, (tile, tile), 1) <= lax.broadcasted_iota(
        jnp.int32, (tile, tile), 0
    )
    scale = HD ** (-0.5)

    def attend(qk, value, valid):
        allowed = causal & (jnp.broadcast_to(valid, causal.shape) > 0.5)
        qk, value = qk.astype(BF), value.astype(BF)
        query, key = qk[:, 0:HD], qk[:, HD : 2 * HD]
        scores = jnp.where(allowed, nt(query, key) * scale, -1e30)
        expo = jnp.exp(scores - jnp.max(scores, -1, keepdims=True))
        prob = expo / jnp.sum(expo, -1, keepdims=True)
        probb = prob.astype(BF)
        attn = nn(probb, value).astype(BF)
        return query, key, value, prob, probb, attn

    def swap_out(name, term):
        e = EXCHANGES.index(name)

        @functools.partial(loop, 0, chunks)
        def _(j):
            own_x[e, j] = term(col(j)).astype(BF)
            for o in range(1, contexts):
                send((name, o, j), own_x.at[e, j], got_x.at[e, contexts - o - 1, j], ctx_peer(o))

    def swap_in(name, j):
        e = EXCHANGES.index(name)
        total = own_x[e, j].astype(F32)
        for o in range(1, contexts):
            slot = contexts - o - 1
            arrive((name, o, j), got_x.at[e, slot, j])
            total = total + got_x[e, slot, j].astype(F32)
        return total

    def backward(keep, dattn):
        query, key, value, prob, probb, attn = keep
        delta = jnp.sum(dattn.astype(F32) * attn.astype(F32), -1, keepdims=True)
        dscore = (prob * (nt(dattn, value) - delta) * scale).astype(BF)
        dq = nn(dscore, key).astype(BF)
        dk = nn(dscore.T, query).astype(BF)
        dv = nn(probb.T, dattn).astype(BF)
        return jnp.concatenate([dq, dk], axis=1), dv

    keep2 = attend(accA[...], accB[0:tile, 0:HD], valid2)
    swap_out("mix2", lambda c: nn(keep2[5], WBT[HD : 2 * HD, c]))
    grad_out3 = accB[tile : 2 * tile, HD : 2 * HD]
    dattn3 = (grad_out3 * valid3).astype(BF)

    def take_mix2(j, carry):
        square, qk, vo = carry
        c = col(j)
        state = (hL[:, c].astype(F32) + swap_in("mix2", j)).astype(BF)
        h2[:, c] = state
        wide = state.astype(F32)
        gained = (wide * gain[:, c]).astype(BF)
        return (
            square + jnp.sum(wide * wide, -1, keepdims=True),
            qk + nn(gained, WA[c, :]),
            vo + nn(jnp.concatenate([gained, state], axis=0), WB[c, :]),
        )

    square, qk3, vo3 = lax.fori_loop(
        0, chunks, take_mix2,
        (no_rows, jnp.zeros((tile, 2 * HD), F32), jnp.zeros((2 * tile, 2 * HD), F32)),
    )
    inv3 = lax.rsqrt(square * (1.0 / D) + 1e-06)
    state_out = vo3[tile : 2 * tile, HD : 2 * HD]

    factor3 = inv3 * valid3
    keep3 = attend(qk3 * factor3, vo3[0:tile, 0:HD] * factor3, valid3)
    dqk3, dv3 = backward(keep3, dattn3)
    swap_out("dn3", lambda c: nn(dqk3, WAT[:, c]) + nn(dv3, WBT[0:HD, c]))
    swap_out("mix3", lambda c: nn(keep3[5], WBT[HD : 2 * HD, c]))

    @functools.partial(loop, 0, chunks)
    def _(j):
        c = col(j)
        R[tile : 2 * tile, c] = (h2[:, c].astype(F32) * inv3 * gain[:, c] * valid3).astype(BF)

    def norm_grad(name, state, inv, on, start, term):
        def step(j, carry):
            dot, back = carry
            c = col(j)
            u = swap_in(name, j) * gain[:, c]
            scaled[:, c] = u
            return dot + jnp.sum(u * state[:, c].astype(F32), -1, keepdims=True), term(c, u, back)

        dot, back = lax.fori_loop(0, chunks, step, (no_rows, start))
        return inv * on, inv * inv * inv * (dot * (1.0 / D)) * on, back

    def norm_apply(state, c, first, second):
        return scaled[:, c] * first - state[:, c].astype(F32) * second

    first3, second3, back = norm_grad(
        "dn3", h2, inv3, valid3, jnp.zeros((tile, HD), F32),
        lambda c, u, back: back + nn(u.astype(BF), WB[c, HD : 2 * HD]),
    )
    dattn2 = (grad_out3 + back * first3 - state_out * second3).astype(BF)
    dqk2, dv2 = backward(keep2, dattn2)

    @functools.partial(loop, 0, chunks)
    def _(j):
        c = col(j)
        DY[0:tile, c] = (DY[0:tile, c].astype(F32) + norm_apply(h2, c, first3, second3)).astype(BF)

    left_a = jnp.concatenate([dqk2, dqk3], axis=0).T
    left_v = jnp.concatenate([dv2, dv3], axis=0).T
    left_o = jnp.concatenate([keep2[5], keep3[5]], axis=0).T
    plane = Y * X

    def cut(rows, block, z):
        for i in range(plane):
            G[z * plane + i, rows, :] = block[:, i * dloc : (i + 1) * dloc].astype(BF)

    got1, got2, sum1 = (R1a, R1b), (R2a, R2b), (T1a, T1b)

    def half_rows(h):
        return pl.ds(h * 2 * HD, 2 * HD)

    def nth(i):
        return jnp.where(2 * zz < Z, Z - 1 - i, lax.rem(i + 1, Z))

    @functools.partial(loop, 0, Z)
    def _(i):
        oz = nth(i)
        g = group_of(oz)
        z = lax.rem(zz + oz, Z)
        cut(pl.ds(0, 2 * HD), nn(left_a, R[:, g]), z)
        cut(pl.ds(2 * HD, HD), nn(left_v, R[:, g]), z)
        cut(pl.ds(3 * HD, HD), nn(left_o, DY[:, g]), z)
        for o2 in reversed(range(max(X, Y))):
            for h in range(2):
                e2, e1 = order[h]
                for o1 in range(1, dims[e1] if o2 < dims[e2] else 1):
                    send(
                        ("s1", h, o1, o2, oz),
                        G.at[at([(0, oz), (e1, o1), (e2, o2)]), half_rows(h), :],
                        got1[h].at[o1 - 1, o2, oz],
                        (at([(e1, o1)]), ctx),
                    )
    swap_out("dn2", lambda c: nn(dqk2, WAT[:, c]) + nn(dv2, WBT[0:HD, c]))

    def first_total(h, o2, oz):
        e2, e1 = order[h]
        total = G[at([(0, oz), (e2, o2)]), half_rows(h), :].astype(F32)
        for o1 in range(1, dims[e1]):
            arrive(("s1", h, o1, o2, oz), got1[h].at[o1 - 1, o2, oz])
            total = total + got1[h][o1 - 1, o2, oz].astype(F32)
        return total

    def second_phase(oz):
        for h in range(2):
            e2, e1 = order[h]
            for o2 in range(1, dims[e2]):
                sum1[h][o2 - 1, oz] = first_total(h, o2, oz).astype(BF)
                send(
                    ("s2", h, o2, oz), sum1[h].at[o2 - 1, oz], got2[h].at[o2 - 1, oz],
                    (at([(e2, o2)]), ctx),
                )

    def second_total(h, oz):
        total = first_total(h, 0, oz)
        for o2 in range(1, dims[order[h][0]]):
            arrive(("s2", h, o2, oz), got2[h].at[o2 - 1, oz])
            total = total + got2[h][o2 - 1, oz].astype(F32)
        return total

    def third_phase(oz):
        for h in range(2):
            T2[h, oz - 1] = second_total(h, oz).astype(BF)
            send(("s3", h, oz), T2.at[h, oz - 1], R3.at[h, oz - 1], (at([(0, oz)]), ctx))

    second_phase(nth(0))

    @functools.partial(loop, 1, Z)
    def _(i):
        second_phase(nth(i))
        third_phase(nth(i - 1))

    not2 = 1.0 - own2

    @functools.partial(loop, 0, chunks)
    def _(j):
        c = col(j)
        state = (h2[:, c].astype(F32) + swap_in("mix3", j)).astype(BF).astype(F32)
        hout[0, :, c] = (hid[0, :, c].astype(F32) * not2 + state * own2).astype(BF)

    first2, second2, _ = norm_grad("dn2", hL, inv2, 1.0, 0, lambda c, u, back: back)

    @functools.partial(loop, 0, chunks)
    def _(j):
        c = col(j)
        grad = DY[0:tile, c].astype(F32) + norm_apply(hL, c, first2, second2)
        grad = grad.astype(BF).astype(F32)
        gout[0, :, c] = (cot[0, :, c].astype(F32) * not2 + grad * own2).astype(BF)

    final = [second_total(h, 0) for h in range(2)]
    for h in range(2):
        for oz in range(1, Z):
            arrive(("s3", h, oz), R3.at[h, oz - 1])
            final[h] = final[h] + R3[h, oz - 1].astype(F32)
    gqkv[0] = final[0][0:HD].T
    gqkv[1] = final[0][HD : 2 * HD].T
    gqkv[2] = final[1][0:HD].T
    gwo[...] = final[1][HD : 2 * HD]

    def sent(kinds, block, half=None):
        numbers = [
            number for key, number in keys.items() if key[0] in kinds and half in (None, key[1])
        ]
        if numbers:
            loop(min(numbers), max(numbers) + 1, lambda k: copy(k, block, block, (dp, ctx)).wait_send())

    sent(("hid", "cot"), hid.at[0])
    sent(EXCHANGES, own_x.at[0, 0])
    for h in range(2):
        sent(("g1", "g2"), piece(0, []), h)

    def line_sent(way, step, on):
        @pl.when(on)
        def _():
            for h in range(2):
                copy(number_of((way, h, step)), piece(h, []), piece(h, []), (dp, ctx)).wait_send()

    @functools.partial(loop, 0, Z - 1)
    def _(step):
        line_sent("up", step, (zz >= step) & (zz < Z - 1))
        line_sent("down", step, (zz + step <= Z - 1) & (zz > 0))

    sent(("s1", "s2", "s3"), T2.at[0, 0])


def write_out(*refs):
    sources, targets, sems = refs[:4], refs[4:8], refs[8]
    copies = [pltpu.make_async_copy(sources[i], targets[i], sems.at[i]) for i in range(4)]
    for c in copies:
        c.start()
    for c in copies:
        c.wait()


def on_device(hidden_in, cotangent, tile_depth, w_qkv, w_out, gain):
    contexts = lax.axis_size("context")
    n = lax.axis_size("dp")
    dims = grid_of(n)
    Z, Y, X = dims
    _, tile, D = hidden_in.shape
    dloc = w_qkv.shape[1]
    chunks = 4
    width = D // chunks
    keys = copy_keys(dims, contexts, chunks)
    others = max(1, contexts - 1)
    vmem = pl.BlockSpec(memory_space=pltpu.VMEM)

    def block(*lead):
        return pltpu.VMEM((*[max(1, v) for v in lead], 2 * HD, dloc), BF)

    results = pl.pallas_call(
        functools.partial(kernel, dims, contexts, chunks, keys),
        out_shape=(
            jax.ShapeDtypeStruct(hidden_in.shape, BF),
            jax.ShapeDtypeStruct(cotangent.shape, BF),
            jax.ShapeDtypeStruct(w_qkv.shape, F32),
            jax.ShapeDtypeStruct(w_out.shape, F32),
        ),
        in_specs=[pl.BlockSpec(memory_space=pltpu.SMEM)] + [vmem] * 5,
        out_specs=(vmem,) * 4,
        scratch_shapes=[
            pltpu.VMEM((D, 2 * HD), BF),
            pltpu.VMEM((D, 2 * HD), BF),
            pltpu.VMEM((2 * HD, D), BF),
            pltpu.VMEM((2 * HD, D), BF),
            pltpu.VMEM((tile, 2 * HD), F32),
            pltpu.VMEM((2 * tile, 2 * HD), F32),
            pltpu.VMEM((others, tile, D), BF),
            pltpu.VMEM((others, tile, D), BF),
            pltpu.VMEM((tile, D), BF),
            pltpu.VMEM((tile, D), BF),
            pltpu.VMEM((2 * tile, D), BF),
            pltpu.VMEM((2 * tile, D), BF),
            pltpu.VMEM((tile, D), F32),
            pltpu.VMEM((len(EXCHANGES), chunks, tile, width), BF),
            pltpu.VMEM((len(EXCHANGES), others, chunks, tile, width), BF),
            pltpu.VMEM((n, 4 * HD, dloc), BF),
            block(Y - 1, X, Z),
            block(X - 1, Y, Z),
            block(X - 1, Z),
            block(Y - 1, Z),
            block(2, Z - 1),
            block(X - 1, Z),
            block(Y - 1, Z),
            block(2, Z - 1),
            pltpu.SemaphoreType.DMA((len(keys),)),
            pltpu.SemaphoreType.DMA((len(keys),)),
        ],
        compiler_params=pltpu.CompilerParams(
            collective_id=0, has_side_effects=True, vmem_limit_bytes=60 * 1024 * 1024
        ),
        cost_estimate=pl.CostEstimate(
            flops=16 * tile * D * 3 * HD, bytes_accessed=8 * tile * D, transcendentals=tile * tile
        ),
        name="recursion_sublayer",
    )(tile_depth, hidden_in, cotangent, w_qkv, w_out, gain[None, :])
    return pl.pallas_call(
        write_out,
        out_shape=tuple(jax.ShapeDtypeStruct(r.shape, r.dtype) for r in results),
        in_specs=[vmem] * 4,
        out_specs=(pl.BlockSpec(memory_space=pl.ANY),) * 4,
        scratch_shapes=[pltpu.SemaphoreType.DMA((4,))],
        name="write_outputs",
    )(*results)


def solution(mesh):
    in_specs = (
        P("dp", "context", None),
        P("dp", "context", None),
        P("dp", None),
        P(None, "dp", "context"),
        P("context", "dp"),
        P(),
    )
    out_specs = (
        P("dp", "context", None),
        P("dp", "context", None),
        P(None, "dp", "context"),
        P("context", "dp"),
    )
    return jax.shard_map(
        on_device, mesh=mesh, in_specs=in_specs, out_specs=out_specs, check_vma=False
    )
```

```python
import functools

import jax
import jax.numpy as jnp
from jax import lax
from jax.experimental import pallas as pl
from jax.experimental.pallas import tpu as pltpu
from jax.sharding import PartitionSpec as P

HD = 128
MESH = pl.DeviceIdType.MESH
BF = jnp.bfloat16
F32 = jnp.float32
EXCHANGES = ("mix2", "mix3", "dn3", "dn2")


def grid_of(n):
    if n == 64:
        return (16, 4, 1)
    if n % 4 == 0:
        return (n // 4, 2, 2)
    return (n, 1, 1)


def copy_keys(dims, contexts, chunks):
    Z, Y, X = dims
    first = (X, Y)
    second = (Y, X)
    keys = [(name, o) for o in range(1, contexts) for name in ("hid", "cot")]
    keys += [(n, o, j) for n in EXCHANGES for o in range(1, contexts) for j in range(chunks)]
    for h in range(2):
        keys += [("gz", h, oz) for oz in range(1, Z)]
        keys += [(way, h, step) for way in ("up", "down") for step in range(Z - 1)]
        keys += [("g1", h, o1, oz) for o1 in range(1, first[h]) for oz in range(Z)]
        keys += [
            ("g2", h, o2, o1, oz)
            for o2 in range(1, second[h])
            for o1 in range(first[h])
            for oz in range(Z)
        ]
    for h in range(2):
        keys += [
            ("s1", h, o1, o2, oz)
            for o1 in range(1, second[h])
            for o2 in range(first[h])
            for oz in range(Z)
        ]
        keys += [("s2", h, o2, oz) for o2 in range(1, first[h]) for oz in range(Z)]
        keys += [("s3", h, oz) for oz in range(1, Z)]
    return {key: number for number, key in enumerate(keys)}


def nn(a, b):
    return jnp.dot(a, b, preferred_element_type=F32)


def nt(a, b):
    return lax.dot_general(a, b, (((1,), (1,)), ((), ())), preferred_element_type=F32)


def kernel(
    dims, contexts, chunks, keys,
    depth_in, hid_in, cot_in, wq_in, wo_in, gain_in,
    hout, gout, gqkv, gwo,
    WA, WB, WAT, WBT, accA, accB, peer_h, peer_g, hL, h2, R, DY, scaled, own_x, got_x,
    G, R1a, R1b, R2a, R2b, R3, T1a, T1b, T2, depth, hid, cot, wq, wo, gain, load_sem, send_sem, recv_sem,
):
    loads = [
        pltpu.make_async_copy(source, target, load_sem.at[i])
        for i, (source, target) in enumerate((
            (wq_in, wq), (wo_in, wo), (hid_in, hid), (cot_in, cot), (gain_in, gain), (depth_in, depth),
        ))
    ]
    for load in loads:
        load.start()
    Z, Y, X = dims
    dp = lax.axis_index("dp")
    ctx = lax.axis_index("context")
    zz, yy, xx = dp // (Y * X), lax.rem(dp // X, Y), lax.rem(dp, X)
    tile, D = hid.shape[1], hid.shape[2]
    dloc = wq.shape[1]
    width = D // chunks
    me = (zz, yy, xx)
    order = ((2, 1), (1, 2))

    def spot(**moves):
        place = list(me)
        for name, off in moves.items():
            axis = int(name[1])
            if not (isinstance(off, int) and off == 0):
                place[axis] = lax.rem(me[axis] + off + dims[axis], dims[axis])
        return (place[0] * Y + place[1]) * X + place[2]

    def at(axes):
        return spot(**{"a%d" % axis: off for axis, off in axes})

    def number_of(key):
        low = 0 if (*key[:-1], 0) in keys else 1
        return keys[(*key[:-1], low)] + (key[-1] - low)

    def copy(number, src, dst, peer, leaving=None):
        leaving = number if leaving is None else leaving
        return pltpu.make_async_remote_copy(
            src_ref=src, dst_ref=dst, send_sem=send_sem.at[leaving], recv_sem=recv_sem.at[number],
            device_id=peer, device_id_type=MESH,
        )

    def send(key, src, dst, peer, leaving=None):
        leaving = None if leaving is None else number_of(leaving)
        copy(number_of(key), src, dst, peer, leaving).start()

    def loop(low, high, body):
        def step(i, carry):
            body(i)
            return carry

        if high > low:
            lax.fori_loop(low, high, step, 0)

    def arrive(key, dst):
        copy(number_of(key), dst, dst, (dp, ctx)).wait_recv()

    def ctx_peer(o):
        return (dp, lax.rem(ctx + o, contexts))

    barrier = pltpu.get_barrier_semaphore()
    peers = [(at([(axis, o)]), ctx) for axis in range(3) for o in range(1, dims[axis])]
    peers += [ctx_peer(o) for o in range(1, contexts)]
    for peer in peers:
        pl.semaphore_signal(barrier, inc=1, device_id=peer, device_id_type=MESH)

    loads[0].wait()
    loads[1].wait()
    mine = pl.ds(pl.multiple_of(dp * dloc, dloc), dloc)
    WA[mine, 0:HD] = wq[0]
    WA[mine, HD : 2 * HD] = wq[1]
    WB[mine, 0:HD] = wq[2]
    WB[mine, HD : 2 * HD] = wo[...].T
    pl.semaphore_wait(barrier, len(peers))

    halves = (WA, WB)

    def piece(h, axes):
        p = at(axes)
        return halves[h].at[pl.ds(pl.multiple_of(p * dloc, dloc), dloc), :]

    def line_up(h, step):
        @pl.when((zz >= step) & (zz < Z - 1))
        def _():
            block = piece(h, [(0, -step)])
            send(("gz", h, step + 1), block, block, (at([(0, 1)]), ctx), ("up", h, step))

    def line_down(h, step):
        @pl.when((zz + step <= Z - 1) & (zz > 0))
        def _():
            block = piece(h, [(0, step)])
            send(("gz", h, Z - 1 - step), block, block, (at([(0, -1)]), ctx), ("down", h, step))

    def spread_first(h, oz):
        d1 = order[h][0]
        block = piece(h, [(0, -oz)])
        for o1 in range(1, dims[d1]):
            send(("g1", h, o1, oz), block, block, (at([(d1, o1)]), ctx))

    def spread_second(h, oz, o1):
        d1, d2 = order[h]
        block = piece(h, [(0, -oz), (d1, -o1)])
        if o1:
            arrive(("g1", h, o1, oz), block)
        for o2 in range(1, dims[d2]):
            send(("g2", h, o2, o1, oz), block, block, (at([(d2, o2)]), ctx))

    def pass_on(oz):
        for h in range(2):
            for o1 in range(1, dims[order[h][0]]):
                spread_second(h, oz, o1)

    for h in range(2):
        spread_first(h, 0)
        if Z > 1:
            line_up(h, 0)
            line_down(h, 0)
    for h in range(2):
        spread_second(h, 0, 0)
    for load in loads[2:]:
        load.wait()
    for o in range(1, contexts):
        slot = contexts - o - 1
        send(("hid", o), hid.at[0], peer_h.at[slot], ctx_peer(o))
        send(("cot", o), cot.at[0], peer_g.at[slot], ctx_peer(o))

    def from_z(oz, step, line):
        for h in range(2):
            arrive(("gz", h, oz), piece(h, [(0, -oz)]))
            spread_first(h, oz)

            @pl.when(step < Z - 1)
            def _(h=h):
                line(h, step)

        for h in range(2):
            spread_second(h, oz, 0)

    def both_ways(step, act):
        @pl.when(zz >= step)
        def _():
            act(step, line_up)

        @pl.when(zz + step <= Z - 1)
        def _():
            act(Z - step, line_down)

    pass_on(0)

    def z_step(step):
        both_ways(step, lambda oz, line: from_z(oz, step, line))
        both_ways(step, lambda oz, line: pass_on(oz))

    loop(1, min(2, Z), z_step)

    tiles = depth.shape[1]

    def flag(level, place):
        return jnp.where(depth[0, place] >= level, 1.0, 0.0).astype(F32)

    def of(level, who):
        return sum(jnp.where(who == t, flag(level, t), 0.0) for t in range(tiles))

    own2 = of(2, ctx)
    valid2 = sum(flag(2, t) for t in range(tiles))
    valid3 = sum(flag(3, t) for t in range(tiles))
    for o in range(1, contexts):
        slot = contexts - o - 1
        arrive(("hid", o), peer_h.at[slot])
        arrive(("cot", o), peer_g.at[slot])
    no_rows = jnp.zeros((tile, 1), F32)

    def col(j):
        return pl.ds(pl.multiple_of(j * width, HD), width)

    def take_live(j, square):
        c = col(j)
        live_h = hid[0, :, c].astype(F32) * own2
        live_g = cot[0, :, c].astype(F32) * own2
        for s in range(contexts - 1):
            flag_s = of(2, lax.rem(ctx + s + 1, contexts))
            live_h = live_h + peer_h[s, :, c].astype(F32) * flag_s
            live_g = live_g + peer_g[s, :, c].astype(F32) * flag_s
        hL[:, c] = live_h.astype(BF)
        DY[0:tile, c] = live_g.astype(BF)
        DY[tile : 2 * tile, c] = (live_g * valid3).astype(BF)
        return square + jnp.sum(live_h * live_h, -1, keepdims=True)

    square = lax.fori_loop(0, chunks, take_live, no_rows)
    inv2 = lax.rsqrt(square * (1.0 / D) + 1e-06)

    @functools.partial(loop, 0, chunks)
    def _(j):
        c = col(j)
        R[0:tile, c] = (hL[:, c].astype(F32) * inv2 * gain[:, c]).astype(BF)

    loop(2, Z, z_step)

    group = D // Z

    def group_of(oz):
        return pl.ds(pl.multiple_of(lax.rem(zz + oz + Z, Z) * group, group), group)

    accA[...] = jnp.zeros_like(accA)
    accB[...] = jnp.zeros_like(accB)

    def project(oz):
        for h in range(2):
            d1, d2 = order[h]
            for o1 in range(dims[d1]):
                for o2 in range(1, dims[d2]):
                    arrive(("g2", h, o2, o1, oz), piece(h, [(0, -oz), (d1, -o1), (d2, -o2)]))
        g = group_of(-oz)
        rows, grads = R[0:tile, g], DY[0:tile, g]
        accA[...] += nn(rows, WA[g, :])
        accB[...] += nn(jnp.concatenate([rows, grads], axis=0), WB[g, :])
        WAT[:, g] = WA[g, :].T
        WBT[:, g] = WB[g, :].T

    project(0)

    @functools.partial(loop, 1, Z)
    def _(step):
        both_ways(step, lambda oz, line: project(oz))

    causal = lax.broadcasted_iota(jnp.int32, (tile, tile), 1) <= lax.broadcasted_iota(
        jnp.int32, (tile, tile), 0
    )
    scale = HD ** (-0.5)

    def attend(qk, value, valid):
        allowed = causal & (jnp.broadcast_to(valid, causal.shape) > 0.5)
        qk, value = qk.astype(BF), value.astype(BF)
        query, key = qk[:, 0:HD], qk[:, HD : 2 * HD]
        scores = jnp.where(allowed, nt(query, key) * scale, -1e30)
        expo = jnp.exp(scores - jnp.max(scores, -1, keepdims=True))
        prob = expo / jnp.sum(expo, -1, keepdims=True)
        probb = prob.astype(BF)
        attn = nn(probb, value).astype(BF)
        return query, key, value, prob, probb, attn

    def swap_out(name, term):
        e = EXCHANGES.index(name)

        @functools.partial(loop, 0, chunks)
        def _(j):
            own_x[e, j] = term(col(j)).astype(BF)
            for o in range(1, contexts):
                send((name, o, j), own_x.at[e, j], got_x.at[e, contexts - o - 1, j], ctx_peer(o))

    def swap_in(name, j):
        e = EXCHANGES.index(name)
        total = own_x[e, j].astype(F32)
        for o in range(1, contexts):
            slot = contexts - o - 1
            arrive((name, o, j), got_x.at[e, slot, j])
            total = total + got_x[e, slot, j].astype(F32)
        return total

    def backward(keep, dattn):
        query, key, value, prob, probb, attn = keep
        delta = jnp.sum(dattn.astype(F32) * attn.astype(F32), -1, keepdims=True)
        dscore = (prob * (nt(dattn, value) - delta) * scale).astype(BF)
        dq = nn(dscore, key).astype(BF)
        dk = nn(dscore.T, query).astype(BF)
        dv = nn(probb.T, dattn).astype(BF)
        return jnp.concatenate([dq, dk], axis=1), dv

    keep2 = attend(accA[...], accB[0:tile, 0:HD], valid2)
    swap_out("mix2", lambda c: nn(keep2[5], WBT[HD : 2 * HD, c]))
    grad_out3 = accB[tile : 2 * tile, HD : 2 * HD]
    dattn3 = (grad_out3 * valid3).astype(BF)

    def take_mix2(j, carry):
        square, qk, vo = carry
        c = col(j)
        state = (hL[:, c].astype(F32) + swap_in("mix2", j)).astype(BF)
        h2[:, c] = state
        wide = state.astype(F32)
        gained = (wide * gain[:, c]).astype(BF)
        return (
            square + jnp.sum(wide * wide, -1, keepdims=True),
            qk + nn(gained, WA[c, :]),
            vo + nn(jnp.concatenate([gained, state], axis=0), WB[c, :]),
        )

    square, qk3, vo3 = lax.fori_loop(
        0, chunks, take_mix2,
        (no_rows, jnp.zeros((tile, 2 * HD), F32), jnp.zeros((2 * tile, 2 * HD), F32)),
    )
    inv3 = lax.rsqrt(square * (1.0 / D) + 1e-06)
    state_out = vo3[tile : 2 * tile, HD : 2 * HD]

    factor3 = inv3 * valid3
    keep3 = attend(qk3 * factor3, vo3[0:tile, 0:HD] * factor3, valid3)
    dqk3, dv3 = backward(keep3, dattn3)
    swap_out("dn3", lambda c: nn(dqk3, WAT[:, c]) + nn(dv3, WBT[0:HD, c]))

    @functools.partial(loop, 0, chunks)
    def _(j):
        c = col(j)
        R[tile : 2 * tile, c] = (h2[:, c].astype(F32) * inv3 * gain[:, c] * valid3).astype(BF)

    def norm_grad(name, state, inv, on, start, term):
        def step(j, carry):
            dot, back = carry
            c = col(j)
            u = swap_in(name, j) * gain[:, c]
            scaled[:, c] = u
            return dot + jnp.sum(u * state[:, c].astype(F32), -1, keepdims=True), term(c, u, back)

        dot, back = lax.fori_loop(0, chunks, step, (no_rows, start))
        return inv * on, inv * inv * inv * (dot * (1.0 / D)) * on, back

    def norm_apply(state, c, first, second):
        return scaled[:, c] * first - state[:, c].astype(F32) * second

    first3, second3, back = norm_grad(
        "dn3", h2, inv3, valid3, jnp.zeros((tile, HD), F32),
        lambda c, u, back: back + nn(u.astype(BF), WB[c, HD : 2 * HD]),
    )
    dattn2 = (grad_out3 + back * first3 - state_out * second3).astype(BF)
    dqk2, dv2 = backward(keep2, dattn2)

    @functools.partial(loop, 0, chunks)
    def _(j):
        c = col(j)
        DY[0:tile, c] = (DY[0:tile, c].astype(F32) + norm_apply(h2, c, first3, second3)).astype(BF)

    left_a = jnp.concatenate([dqk2, dqk3], axis=0).T
    left_v = jnp.concatenate([dv2, dv3], axis=0).T
    left_o = jnp.concatenate([keep2[5], keep3[5]], axis=0).T
    plane = Y * X

    def cut(rows, block, z):
        for i in range(plane):
            G[z * plane + i, rows, :] = block[:, i * dloc : (i + 1) * dloc].astype(BF)

    got1, got2, sum1 = (R1a, R1b), (R2a, R2b), (T1a, T1b)

    def half_rows(h):
        return pl.ds(h * 2 * HD, 2 * HD)

    def nth(i):
        return jnp.where(2 * zz < Z, Z - 1 - i, lax.rem(i + 1, Z))

    @functools.partial(loop, 0, Z)
    def _(i):
        oz = nth(i)
        g = group_of(oz)
        z = lax.rem(zz + oz, Z)
        cut(pl.ds(0, 2 * HD), nn(left_a, R[:, g]), z)
        cut(pl.ds(2 * HD, HD), nn(left_v, R[:, g]), z)
        cut(pl.ds(3 * HD, HD), nn(left_o, DY[:, g]), z)
        for o2 in reversed(range(max(X, Y))):
            for h in range(2):
                e2, e1 = order[h]
                for o1 in range(1, dims[e1] if o2 < dims[e2] else 1):
                    send(
                        ("s1", h, o1, o2, oz),
                        G.at[at([(0, oz), (e1, o1), (e2, o2)]), half_rows(h), :],
                        got1[h].at[o1 - 1, o2, oz],
                        (at([(e1, o1)]), ctx),
                    )
    swap_out("mix3", lambda c: nn(keep3[5], WBT[HD : 2 * HD, c]))
    swap_out("dn2", lambda c: nn(dqk2, WAT[:, c]) + nn(dv2, WBT[0:HD, c]))

    def first_total(h, o2, oz):
        e2, e1 = order[h]
        total = G[at([(0, oz), (e2, o2)]), half_rows(h), :].astype(F32)
        for o1 in range(1, dims[e1]):
            arrive(("s1", h, o1, o2, oz), got1[h].at[o1 - 1, o2, oz])
            total = total + got1[h][o1 - 1, o2, oz].astype(F32)
        return total

    def second_phase(oz):
        for h in range(2):
            e2, e1 = order[h]
            for o2 in range(1, dims[e2]):
                sum1[h][o2 - 1, oz] = first_total(h, o2, oz).astype(BF)
                send(
                    ("s2", h, o2, oz), sum1[h].at[o2 - 1, oz], got2[h].at[o2 - 1, oz],
                    (at([(e2, o2)]), ctx),
                )

    def second_total(h, oz):
        total = first_total(h, 0, oz)
        for o2 in range(1, dims[order[h][0]]):
            arrive(("s2", h, o2, oz), got2[h].at[o2 - 1, oz])
            total = total + got2[h][o2 - 1, oz].astype(F32)
        return total

    def third_phase(oz):
        for h in range(2):
            T2[h, oz - 1] = second_total(h, oz).astype(BF)
            send(("s3", h, oz), T2.at[h, oz - 1], R3.at[h, oz - 1], (at([(0, oz)]), ctx))

    second_phase(nth(0))

    @functools.partial(loop, 1, Z)
    def _(i):
        second_phase(nth(i))
        third_phase(nth(i - 1))

    not2 = 1.0 - own2

    @functools.partial(loop, 0, chunks)
    def _(j):
        c = col(j)
        state = (h2[:, c].astype(F32) + swap_in("mix3", j)).astype(BF).astype(F32)
        hout[0, :, c] = (hid[0, :, c].astype(F32) * not2 + state * own2).astype(BF)

    first2, second2, _ = norm_grad("dn2", hL, inv2, 1.0, 0, lambda c, u, back: back)

    @functools.partial(loop, 0, chunks)
    def _(j):
        c = col(j)
        grad = DY[0:tile, c].astype(F32) + norm_apply(hL, c, first2, second2)
        grad = grad.astype(BF).astype(F32)
        gout[0, :, c] = (cot[0, :, c].astype(F32) * not2 + grad * own2).astype(BF)

    final = [second_total(h, 0) for h in range(2)]
    for h in range(2):
        for oz in range(1, Z):
            arrive(("s3", h, oz), R3.at[h, oz - 1])
            final[h] = final[h] + R3[h, oz - 1].astype(F32)
    gqkv[0] = final[0][0:HD].T
    gqkv[1] = final[0][HD : 2 * HD].T
    gqkv[2] = final[1][0:HD].T
    gwo[...] = final[1][HD : 2 * HD]

    def sent(kinds, block, half=None):
        numbers = [
            number for key, number in keys.items() if key[0] in kinds and half in (None, key[1])
        ]
        if numbers:
            loop(min(numbers), max(numbers) + 1, lambda k: copy(k, block, block, (dp, ctx)).wait_send())

    sent(("hid", "cot"), hid.at[0])
    sent(EXCHANGES, own_x.at[0, 0])
    for h in range(2):
        sent(("g1", "g2"), piece(0, []), h)

    def line_sent(way, step, on):
        @pl.when(on)
        def _():
            for h in range(2):
                copy(number_of((way, h, step)), piece(h, []), piece(h, []), (dp, ctx)).wait_send()

    @functools.partial(loop, 0, Z - 1)
    def _(step):
        line_sent("up", step, (zz >= step) & (zz < Z - 1))
        line_sent("down", step, (zz + step <= Z - 1) & (zz > 0))

    sent(("s1", "s2", "s3"), T2.at[0, 0])


def write_out(*refs):
    sources, targets, sems = refs[:4], refs[4:8], refs[8]
    copies = [pltpu.make_async_copy(sources[i], targets[i], sems.at[i]) for i in range(4)]
    for c in copies:
        c.start()
    for c in copies:
        c.wait()


def on_device(hidden_in, cotangent, tile_depth, w_qkv, w_out, gain):
    contexts = lax.axis_size("context")
    n = lax.axis_size("dp")
    dims = grid_of(n)
    Z, Y, X = dims
    _, tile, D = hidden_in.shape
    dloc = w_qkv.shape[1]
    chunks = 4
    width = D // chunks
    keys = copy_keys(dims, contexts, chunks)
    others = max(1, contexts - 1)
    vmem = pl.BlockSpec(memory_space=pltpu.VMEM)

    def block(*lead):
        return pltpu.VMEM((*[max(1, v) for v in lead], 2 * HD, dloc), BF)

    results = pl.pallas_call(
        functools.partial(kernel, dims, contexts, chunks, keys),
        out_shape=(
            pltpu.VMEM(hidden_in.shape, BF),
            pltpu.VMEM(cotangent.shape, BF),
            pltpu.VMEM(w_qkv.shape, F32),
            pltpu.VMEM(w_out.shape, F32),
        ),
        in_specs=[pl.BlockSpec(memory_space=pltpu.HBM)] * 6,
        out_specs=(vmem,) * 4,
        scratch_shapes=[
            pltpu.VMEM((D, 2 * HD), BF),
            pltpu.VMEM((D, 2 * HD), BF),
            pltpu.VMEM((2 * HD, D), BF),
            pltpu.VMEM((2 * HD, D), BF),
            pltpu.VMEM((tile, 2 * HD), F32),
            pltpu.VMEM((2 * tile, 2 * HD), F32),
            pltpu.VMEM((others, tile, D), BF),
            pltpu.VMEM((others, tile, D), BF),
            pltpu.VMEM((tile, D), BF),
            pltpu.VMEM((tile, D), BF),
            pltpu.VMEM((2 * tile, D), BF),
            pltpu.VMEM((2 * tile, D), BF),
            pltpu.VMEM((tile, D), F32),
            pltpu.VMEM((len(EXCHANGES), chunks, tile, width), BF),
            pltpu.VMEM((len(EXCHANGES), others, chunks, tile, width), BF),
            pltpu.VMEM((n, 4 * HD, dloc), BF),
            block(Y - 1, X, Z),
            block(X - 1, Y, Z),
            block(X - 1, Z),
            block(Y - 1, Z),
            block(2, Z - 1),
            block(X - 1, Z),
            block(Y - 1, Z),
            block(2, Z - 1),
            pltpu.SMEM(tile_depth.shape, jnp.int32),
            pltpu.VMEM(hidden_in.shape, BF),
            pltpu.VMEM(cotangent.shape, BF),
            pltpu.VMEM(w_qkv.shape, BF),
            pltpu.VMEM(w_out.shape, BF),
            pltpu.VMEM((1, D), F32),
            pltpu.SemaphoreType.DMA((6,)),
            pltpu.SemaphoreType.DMA((len(keys),)),
            pltpu.SemaphoreType.DMA((len(keys),)),
        ],
        compiler_params=pltpu.CompilerParams(
            collective_id=0, has_side_effects=True, vmem_limit_bytes=56 * 1024 * 1024
        ),
        cost_estimate=pl.CostEstimate(
            flops=16 * tile * D * 3 * HD, bytes_accessed=8 * tile * D, transcendentals=tile * tile
        ),
        name="recursion_sublayer",
    )(tile_depth, hidden_in, cotangent, w_qkv, w_out, gain[None, :])
    return pl.pallas_call(
        write_out,
        out_shape=tuple(jax.ShapeDtypeStruct(r.shape, r.dtype) for r in results),
        in_specs=[vmem] * 4,
        out_specs=(pl.BlockSpec(memory_space=pl.ANY),) * 4,
        scratch_shapes=[pltpu.SemaphoreType.DMA((4,))],
        name="write_outputs",
    )(*results)


def solution(mesh):
    in_specs = (
        P("dp", "context", None),
        P("dp", "context", None),
        P("dp", None),
        P(None, "dp", "context"),
        P("context", "dp"),
        P(),
    )
    out_specs = (
        P("dp", "context", None),
        P("dp", "context", None),
        P(None, "dp", "context"),
        P("context", "dp"),
    )
    return jax.shard_map(
        on_device, mesh=mesh, in_specs=in_specs, out_specs=out_specs, check_vma=False
    )
```

```python
import functools

import jax
import jax.numpy as jnp
from jax import lax
from jax.experimental import pallas as pl
from jax.experimental.pallas import tpu as pltpu
from jax.sharding import PartitionSpec as P

HD = 128
MESH = pl.DeviceIdType.MESH
BF = jnp.bfloat16
F32 = jnp.float32
EXCHANGES = ("mix2", "mix3", "dn3", "dn2")


def grid_of(n):
    if n == 64:
        return (16, 4, 1)
    if n % 4 == 0:
        return (n // 4, 2, 2)
    return (n, 1, 1)


def copy_keys(dims, contexts, chunks):
    Z, Y, X = dims
    first = (X, Y)
    second = (Y, X)
    keys = [(name, o) for o in range(1, contexts) for name in ("hid", "cot")]
    keys += [(n, o, j) for n in EXCHANGES for o in range(1, contexts) for j in range(chunks)]
    for h in range(2):
        keys += [("gz", h, oz) for oz in range(1, Z)]
        keys += [(way, h, step) for way in ("up", "down") for step in range(Z - 1)]
        keys += [("g1", h, o1, oz) for o1 in range(1, first[h]) for oz in range(Z)]
        keys += [
            ("g2", h, o2, o1, oz)
            for o2 in range(1, second[h])
            for o1 in range(first[h])
            for oz in range(Z)
        ]
    for h in range(2):
        keys += [
            ("s1", h, o1, o2, oz)
            for o1 in range(1, second[h])
            for o2 in range(first[h])
            for oz in range(Z)
        ]
        keys += [("s2", h, o2, oz) for o2 in range(1, first[h]) for oz in range(Z)]
        keys += [("s3", h, oz) for oz in range(1, Z)]
    return {key: number for number, key in enumerate(keys)}


def nn(a, b):
    return jnp.dot(a, b, preferred_element_type=F32)


def nt(a, b):
    return lax.dot_general(a, b, (((1,), (1,)), ((), ())), preferred_element_type=F32)


def kernel(
    dims, contexts, chunks, keys,
    depth_in, hid_in, cot_in, wq_in, wo_in, gain_in,
    hout, gout, gqkv, gwo,
    WA, WB, WAT, WBT, accA, accB, peer_h, peer_g, hL, h2, R, DY, scaled, own_x, got_x,
    G, R1a, R1b, R2a, R2b, R3, T1a, T1b, T2, depth, hid, cot, wq, wo, gain, load_sem, send_sem, recv_sem,
):
    loads = [
        pltpu.make_async_copy(source, target, load_sem.at[i])
        for i, (source, target) in enumerate((
            (wq_in, wq), (wo_in, wo), (hid_in, hid), (cot_in, cot), (gain_in, gain), (depth_in, depth),
        ))
    ]
    for load in loads:
        load.start()
    Z, Y, X = dims
    dp = lax.axis_index("dp")
    ctx = lax.axis_index("context")
    zz, yy, xx = dp // (Y * X), lax.rem(dp // X, Y), lax.rem(dp, X)
    tile, D = hid.shape[1], hid.shape[2]
    dloc = wq.shape[1]
    width = D // chunks
    me = (zz, yy, xx)
    order = ((2, 1), (1, 2))

    def spot(**moves):
        place = list(me)
        for name, off in moves.items():
            axis = int(name[1])
            if not (isinstance(off, int) and off == 0):
                place[axis] = lax.rem(me[axis] + off + dims[axis], dims[axis])
        return (place[0] * Y + place[1]) * X + place[2]

    def at(axes):
        return spot(**{"a%d" % axis: off for axis, off in axes})

    def number_of(key):
        low = 0 if (*key[:-1], 0) in keys else 1
        return keys[(*key[:-1], low)] + (key[-1] - low)

    def copy(number, src, dst, peer, leaving=None):
        leaving = number if leaving is None else leaving
        return pltpu.make_async_remote_copy(
            src_ref=src, dst_ref=dst, send_sem=send_sem.at[leaving], recv_sem=recv_sem.at[number],
            device_id=peer, device_id_type=MESH,
        )

    def send(key, src, dst, peer, leaving=None):
        leaving = None if leaving is None else number_of(leaving)
        copy(number_of(key), src, dst, peer, leaving).start()

    def loop(low, high, body):
        def step(i, carry):
            body(i)
            return carry

        if high > low:
            lax.fori_loop(low, high, step, 0)

    def arrive(key, dst):
        copy(number_of(key), dst, dst, (dp, ctx)).wait_recv()

    def ctx_peer(o):
        return (dp, lax.rem(ctx + o, contexts))

    barrier = pltpu.get_barrier_semaphore()
    peers = [(at([(axis, o)]), ctx) for axis in range(3) for o in range(1, dims[axis])]
    peers += [ctx_peer(o) for o in range(1, contexts)]
    for peer in peers:
        pl.semaphore_signal(barrier, inc=1, device_id=peer, device_id_type=MESH)

    loads[0].wait()
    loads[1].wait()
    mine = pl.ds(pl.multiple_of(dp * dloc, dloc), dloc)
    WA[mine, 0:HD] = wq[0]
    WA[mine, HD : 2 * HD] = wq[1]
    WB[mine, 0:HD] = wq[2]
    WB[mine, HD : 2 * HD] = wo[...].T
    pl.semaphore_wait(barrier, len(peers))

    halves = (WA, WB)

    def piece(h, axes):
        p = at(axes)
        return halves[h].at[pl.ds(pl.multiple_of(p * dloc, dloc), dloc), :]

    def line_up(h, step):
        @pl.when((zz >= step) & (zz < Z - 1))
        def _():
            block = piece(h, [(0, -step)])
            send(("gz", h, step + 1), block, block, (at([(0, 1)]), ctx), ("up", h, step))

    def line_down(h, step):
        @pl.when((zz + step <= Z - 1) & (zz > 0))
        def _():
            block = piece(h, [(0, step)])
            send(("gz", h, Z - 1 - step), block, block, (at([(0, -1)]), ctx), ("down", h, step))

    def spread_first(h, oz):
        d1 = order[h][0]
        block = piece(h, [(0, -oz)])
        for o1 in range(1, dims[d1]):
            send(("g1", h, o1, oz), block, block, (at([(d1, o1)]), ctx))

    def spread_second(h, oz, o1):
        d1, d2 = order[h]
        block = piece(h, [(0, -oz), (d1, -o1)])
        if o1:
            arrive(("g1", h, o1, oz), block)
        for o2 in range(1, dims[d2]):
            send(("g2", h, o2, o1, oz), block, block, (at([(d2, o2)]), ctx))

    def pass_on(oz):
        for h in range(2):
            for o1 in range(1, dims[order[h][0]]):
                spread_second(h, oz, o1)

    for h in range(2):
        spread_first(h, 0)
        if Z > 1:
            line_up(h, 0)
            line_down(h, 0)
    for h in range(2):
        spread_second(h, 0, 0)
    for load in loads[2:]:
        load.wait()
    for o in range(1, contexts):
        slot = contexts - o - 1
        send(("hid", o), hid.at[0], peer_h.at[slot], ctx_peer(o))
        send(("cot", o), cot.at[0], peer_g.at[slot], ctx_peer(o))

    def from_z(oz, step, line):
        for h in range(2):
            arrive(("gz", h, oz), piece(h, [(0, -oz)]))
            spread_first(h, oz)

            @pl.when(step < Z - 1)
            def _(h=h):
                line(h, step)

        for h in range(2):
            spread_second(h, oz, 0)

    def both_ways(step, act):
        @pl.when(zz >= step)
        def _():
            act(step, line_up)

        @pl.when(zz + step <= Z - 1)
        def _():
            act(Z - step, line_down)

    pass_on(0)

    def z_step(step):
        both_ways(step, lambda oz, line: from_z(oz, step, line))
        both_ways(step, lambda oz, line: pass_on(oz))

    loop(1, min(2, Z), z_step)

    tiles = depth.shape[1]

    def flag(level, place):
        return jnp.where(depth[0, place] >= level, 1.0, 0.0).astype(F32)

    def of(level, who):
        return sum(jnp.where(who == t, flag(level, t), 0.0) for t in range(tiles))

    own2 = of(2, ctx)
    valid2 = sum(flag(2, t) for t in range(tiles))
    valid3 = sum(flag(3, t) for t in range(tiles))
    for o in range(1, contexts):
        slot = contexts - o - 1
        arrive(("hid", o), peer_h.at[slot])
        arrive(("cot", o), peer_g.at[slot])
    no_rows = jnp.zeros((tile, 1), F32)

    def col(j):
        return pl.ds(pl.multiple_of(j * width, HD), width)

    def take_live(j, square):
        c = col(j)
        live_h = hid[0, :, c].astype(F32) * own2
        live_g = cot[0, :, c].astype(F32) * own2
        for s in range(contexts - 1):
            flag_s = of(2, lax.rem(ctx + s + 1, contexts))
            live_h = live_h + peer_h[s, :, c].astype(F32) * flag_s
            live_g = live_g + peer_g[s, :, c].astype(F32) * flag_s
        hL[:, c] = live_h.astype(BF)
        DY[0:tile, c] = live_g.astype(BF)
        DY[tile : 2 * tile, c] = (live_g * valid3).astype(BF)
        return square + jnp.sum(live_h * live_h, -1, keepdims=True)

    square = lax.fori_loop(0, chunks, take_live, no_rows)
    inv2 = lax.rsqrt(square * (1.0 / D) + 1e-06)

    @functools.partial(loop, 0, chunks)
    def _(j):
        c = col(j)
        R[0:tile, c] = (hL[:, c].astype(F32) * inv2 * gain[:, c]).astype(BF)

    loop(2, Z, z_step)

    group = D // Z

    def group_of(oz):
        return pl.ds(pl.multiple_of(lax.rem(zz + oz + Z, Z) * group, group), group)

    accA[...] = jnp.zeros_like(accA)
    accB[...] = jnp.zeros_like(accB)

    def project(oz):
        for h in range(2):
            d1, d2 = order[h]
            for o1 in range(dims[d1]):
                for o2 in range(1, dims[d2]):
                    arrive(("g2", h, o2, o1, oz), piece(h, [(0, -oz), (d1, -o1), (d2, -o2)]))
        g = group_of(-oz)
        rows, grads = R[0:tile, g], DY[0:tile, g]
        accA[...] += nn(rows, WA[g, :])
        accB[...] += nn(jnp.concatenate([rows, grads], axis=0), WB[g, :])
        WAT[:, g] = WA[g, :].T
        WBT[:, g] = WB[g, :].T

    project(0)

    @functools.partial(loop, 1, Z)
    def _(step):
        both_ways(step, lambda oz, line: project(oz))

    causal = lax.broadcasted_iota(jnp.int32, (tile, tile), 1) <= lax.broadcasted_iota(
        jnp.int32, (tile, tile), 0
    )
    scale = HD ** (-0.5)

    def attend(qk, value, valid):
        allowed = causal & (jnp.broadcast_to(valid, causal.shape) > 0.5)
        qk, value = qk.astype(BF), value.astype(BF)
        query, key = qk[:, 0:HD], qk[:, HD : 2 * HD]
        scores = jnp.where(allowed, nt(query, key) * scale, -1e30)
        expo = jnp.exp(scores - jnp.max(scores, -1, keepdims=True))
        prob = expo / jnp.sum(expo, -1, keepdims=True)
        probb = prob.astype(BF)
        attn = nn(probb, value).astype(BF)
        return query, key, value, prob, probb, attn

    def swap_out(name, term):
        e = EXCHANGES.index(name)

        @functools.partial(loop, 0, chunks)
        def _(j):
            own_x[e, j] = term(col(j)).astype(BF)
            for o in range(1, contexts):
                send((name, o, j), own_x.at[e, j], got_x.at[e, contexts - o - 1, j], ctx_peer(o))

    def swap_in(name, j):
        e = EXCHANGES.index(name)
        total = own_x[e, j].astype(F32)
        for o in range(1, contexts):
            slot = contexts - o - 1
            arrive((name, o, j), got_x.at[e, slot, j])
            total = total + got_x[e, slot, j].astype(F32)
        return total

    def backward(keep, dattn):
        query, key, value, prob, probb, attn = keep
        delta = jnp.sum(dattn.astype(F32) * attn.astype(F32), -1, keepdims=True)
        dscore = (prob * (nt(dattn, value) - delta) * scale).astype(BF)
        dq = nn(dscore, key).astype(BF)
        dk = nn(dscore.T, query).astype(BF)
        dv = nn(probb.T, dattn).astype(BF)
        return jnp.concatenate([dq, dk], axis=1), dv

    keep2 = attend(accA[...], accB[0:tile, 0:HD], valid2)
    swap_out("mix2", lambda c: nn(keep2[5], WBT[HD : 2 * HD, c]))
    grad_out3 = accB[tile : 2 * tile, HD : 2 * HD]
    dattn3 = (grad_out3 * valid3).astype(BF)

    def take_mix2(j, carry):
        square, qk, vo = carry
        c = col(j)
        state = (hL[:, c].astype(F32) + swap_in("mix2", j)).astype(BF)
        h2[:, c] = state
        wide = state.astype(F32)
        gained = (wide * gain[:, c]).astype(BF)
        return (
            square + jnp.sum(wide * wide, -1, keepdims=True),
            qk + nn(gained, WA[c, :]),
            vo + nn(jnp.concatenate([gained, state], axis=0), WB[c, :]),
        )

    square, qk3, vo3 = lax.fori_loop(
        0, chunks, take_mix2,
        (no_rows, jnp.zeros((tile, 2 * HD), F32), jnp.zeros((2 * tile, 2 * HD), F32)),
    )
    inv3 = lax.rsqrt(square * (1.0 / D) + 1e-06)
    state_out = vo3[tile : 2 * tile, HD : 2 * HD]

    factor3 = inv3 * valid3
    keep3 = attend(qk3 * factor3, vo3[0:tile, 0:HD] * factor3, valid3)
    dqk3, dv3 = backward(keep3, dattn3)
    swap_out("dn3", lambda c: nn(dqk3, WAT[:, c]) + nn(dv3, WBT[0:HD, c]))

    @functools.partial(loop, 0, chunks)
    def _(j):
        c = col(j)
        R[tile : 2 * tile, c] = (h2[:, c].astype(F32) * inv3 * gain[:, c] * valid3).astype(BF)

    def norm_grad(name, state, inv, on, start, term):
        def step(j, carry):
            dot, back = carry
            c = col(j)
            u = swap_in(name, j) * gain[:, c]
            scaled[:, c] = u
            return dot + jnp.sum(u * state[:, c].astype(F32), -1, keepdims=True), term(c, u, back)

        dot, back = lax.fori_loop(0, chunks, step, (no_rows, start))
        return inv * on, inv * inv * inv * (dot * (1.0 / D)) * on, back

    def norm_apply(state, c, first, second):
        return scaled[:, c] * first - state[:, c].astype(F32) * second

    first3, second3, back = norm_grad(
        "dn3", h2, inv3, valid3, jnp.zeros((tile, HD), F32),
        lambda c, u, back: back + nn(u.astype(BF), WB[c, HD : 2 * HD]),
    )
    dattn2 = (grad_out3 + back * first3 - state_out * second3).astype(BF)
    dqk2, dv2 = backward(keep2, dattn2)

    @functools.partial(loop, 0, chunks)
    def _(j):
        c = col(j)
        DY[0:tile, c] = (DY[0:tile, c].astype(F32) + norm_apply(h2, c, first3, second3)).astype(BF)

    left_a = jnp.concatenate([dqk2, dqk3], axis=0).T
    left_v = jnp.concatenate([dv2, dv3], axis=0).T
    left_o = jnp.concatenate([keep2[5], keep3[5]], axis=0).T
    plane = Y * X

    def cut(rows, block, z):
        for i in range(plane):
            G[z * plane + i, rows, :] = block[:, i * dloc : (i + 1) * dloc].astype(BF)

    got1, got2, sum1 = (R1a, R1b), (R2a, R2b), (T1a, T1b)

    def half_rows(h):
        return pl.ds(h * 2 * HD, 2 * HD)

    def nth(i):
        return jnp.where(2 * zz < Z, Z - 1 - i, lax.rem(i + 1, Z))

    @functools.partial(loop, 0, Z)
    def _(i):
        oz = nth(i)
        g = group_of(oz)
        z = lax.rem(zz + oz, Z)
        cut(pl.ds(0, 2 * HD), nn(left_a, R[:, g]), z)
        cut(pl.ds(2 * HD, HD), nn(left_v, R[:, g]), z)
        cut(pl.ds(3 * HD, HD), nn(left_o, DY[:, g]), z)
        for o2 in reversed(range(max(X, Y))):
            for h in range(2):
                e2, e1 = order[h]
                for o1 in range(1, dims[e1] if o2 < dims[e2] else 1):
                    send(
                        ("s1", h, o1, o2, oz),
                        G.at[at([(0, oz), (e1, o1), (e2, o2)]), half_rows(h), :],
                        got1[h].at[o1 - 1, o2, oz],
                        (at([(e1, o1)]), ctx),
                    )
    swap_out("mix3", lambda c: nn(keep3[5], WBT[HD : 2 * HD, c]))
    swap_out("dn2", lambda c: nn(dqk2, WAT[:, c]) + nn(dv2, WBT[0:HD, c]))

    def first_total(h, o2, oz):
        e2, e1 = order[h]
        total = G[at([(0, oz), (e2, o2)]), half_rows(h), :].astype(F32)
        for o1 in range(1, dims[e1]):
            arrive(("s1", h, o1, o2, oz), got1[h].at[o1 - 1, o2, oz])
            total = total + got1[h][o1 - 1, o2, oz].astype(F32)
        return total

    def second_phase(oz):
        for h in range(2):
            e2, e1 = order[h]
            for o2 in range(1, dims[e2]):
                sum1[h][o2 - 1, oz] = first_total(h, o2, oz).astype(BF)
                send(
                    ("s2", h, o2, oz), sum1[h].at[o2 - 1, oz], got2[h].at[o2 - 1, oz],
                    (at([(e2, o2)]), ctx),
                )

    def second_total(h, oz):
        total = first_total(h, 0, oz)
        for o2 in range(1, dims[order[h][0]]):
            arrive(("s2", h, o2, oz), got2[h].at[o2 - 1, oz])
            total = total + got2[h][o2 - 1, oz].astype(F32)
        return total

    def third_phase(oz):
        for h in range(2):
            T2[h, oz - 1] = second_total(h, oz).astype(BF)
            send(("s3", h, oz), T2.at[h, oz - 1], R3.at[h, oz - 1], (at([(0, oz)]), ctx))

    second_phase(nth(0))

    @functools.partial(loop, 1, Z)
    def _(i):
        second_phase(nth(i))
        third_phase(nth(i - 1))

    not2 = 1.0 - own2

    @functools.partial(loop, 0, chunks)
    def _(j):
        c = col(j)
        state = (h2[:, c].astype(F32) + swap_in("mix3", j)).astype(BF).astype(F32)
        hout[0, :, c] = (hid[0, :, c].astype(F32) * not2 + state * own2).astype(BF)

    first2, second2, _ = norm_grad("dn2", hL, inv2, 1.0, 0, lambda c, u, back: back)

    @functools.partial(loop, 0, chunks)
    def _(j):
        c = col(j)
        grad = DY[0:tile, c].astype(F32) + norm_apply(hL, c, first2, second2)
        grad = grad.astype(BF).astype(F32)
        gout[0, :, c] = (cot[0, :, c].astype(F32) * not2 + grad * own2).astype(BF)

    final = [second_total(h, 0) for h in range(2)]
    for h in range(2):
        for oz in range(1, Z):
            arrive(("s3", h, oz), R3.at[h, oz - 1])
            final[h] = final[h] + R3[h, oz - 1].astype(F32)
    gqkv[0] = final[0][0:HD].T
    gqkv[1] = final[0][HD : 2 * HD].T
    gqkv[2] = final[1][0:HD].T
    gwo[...] = final[1][HD : 2 * HD]

    def sent(kinds, block, half=None):
        numbers = [
            number for key, number in keys.items() if key[0] in kinds and half in (None, key[1])
        ]
        if numbers:
            loop(min(numbers), max(numbers) + 1, lambda k: copy(k, block, block, (dp, ctx)).wait_send())

    sent(("hid", "cot"), hid.at[0])
    sent(EXCHANGES, own_x.at[0, 0])
    for h in range(2):
        sent(("g1", "g2"), piece(0, []), h)

    def line_sent(way, step, on):
        @pl.when(on)
        def _():
            for h in range(2):
                copy(number_of((way, h, step)), piece(h, []), piece(h, []), (dp, ctx)).wait_send()

    @functools.partial(loop, 0, Z - 1)
    def _(step):
        line_sent("up", step, (zz >= step) & (zz < Z - 1))
        line_sent("down", step, (zz + step <= Z - 1) & (zz > 0))

    sent(("s1", "s2", "s3"), T2.at[0, 0])


def write_out(*refs):
    sources, targets, sems = refs[:4], refs[4:8], refs[8]
    copies = [pltpu.make_async_copy(sources[i], targets[i], sems.at[i]) for i in range(4)]
    for c in copies:
        c.start()
    for c in copies:
        c.wait()


def on_device(hidden_in, cotangent, tile_depth, w_qkv, w_out, gain):
    contexts = lax.axis_size("context")
    n = lax.axis_size("dp")
    dims = grid_of(n)
    Z, Y, X = dims
    _, tile, D = hidden_in.shape
    dloc = w_qkv.shape[1]
    chunks = 4
    width = D // chunks
    keys = copy_keys(dims, contexts, chunks)
    others = max(1, contexts - 1)
    vmem = pl.BlockSpec(memory_space=pltpu.VMEM)

    def block(*lead):
        return pltpu.VMEM((*[max(1, v) for v in lead], 2 * HD, dloc), BF)

    results = pl.pallas_call(
        functools.partial(kernel, dims, contexts, chunks, keys),
        out_shape=(
            pltpu.VMEM(hidden_in.shape, BF),
            pltpu.VMEM(cotangent.shape, BF),
            pltpu.VMEM(w_qkv.shape, F32),
            pltpu.VMEM(w_out.shape, F32),
        ),
        in_specs=[pl.BlockSpec(memory_space=pltpu.HBM)] * 6,
        out_specs=(vmem,) * 4,
        scratch_shapes=[
            pltpu.VMEM((D, 2 * HD), BF),
            pltpu.VMEM((D, 2 * HD), BF),
            pltpu.VMEM((2 * HD, D), BF),
            pltpu.VMEM((2 * HD, D), BF),
            pltpu.VMEM((tile, 2 * HD), F32),
            pltpu.VMEM((2 * tile, 2 * HD), F32),
            pltpu.VMEM((others, tile, D), BF),
            pltpu.VMEM((others, tile, D), BF),
            pltpu.VMEM((tile, D), BF),
            pltpu.VMEM((tile, D), BF),
            pltpu.VMEM((2 * tile, D), BF),
            pltpu.VMEM((2 * tile, D), BF),
            pltpu.VMEM((tile, D), F32),
            pltpu.VMEM((len(EXCHANGES), chunks, tile, width), BF),
            pltpu.VMEM((len(EXCHANGES), others, chunks, tile, width), BF),
            pltpu.VMEM((n, 4 * HD, dloc), BF),
            block(Y - 1, X, Z),
            block(X - 1, Y, Z),
            block(X - 1, Z),
            block(Y - 1, Z),
            block(2, Z - 1),
            block(X - 1, Z),
            block(Y - 1, Z),
            block(2, Z - 1),
            pltpu.SMEM(tile_depth.shape, jnp.int32),
            pltpu.VMEM(hidden_in.shape, BF),
            pltpu.VMEM(cotangent.shape, BF),
            pltpu.VMEM(w_qkv.shape, BF),
            pltpu.VMEM(w_out.shape, BF),
            pltpu.VMEM((1, D), F32),
            pltpu.SemaphoreType.DMA((6,)),
            pltpu.SemaphoreType.DMA((len(keys),)),
            pltpu.SemaphoreType.DMA((len(keys),)),
        ],
        compiler_params=pltpu.CompilerParams(
            collective_id=0, has_side_effects=True, vmem_limit_bytes=56 * 1024 * 1024
        ),
        cost_estimate=pl.CostEstimate(
            flops=16 * tile * D * 3 * HD, bytes_accessed=8 * tile * D, transcendentals=tile * tile
        ),
        name="recursion_sublayer",
    )(tile_depth, hidden_in, cotangent, w_qkv, w_out, gain[None, :])
    return pl.pallas_call(
        write_out,
        out_shape=tuple(jax.ShapeDtypeStruct(r.shape, r.dtype) for r in results),
        in_specs=[vmem] * 4,
        out_specs=(pl.BlockSpec(memory_space=pl.ANY),) * 4,
        scratch_shapes=[pltpu.SemaphoreType.DMA((4,))],
        compiler_params=pltpu.CompilerParams(vmem_limit_bytes=4 * 1024 * 1024),
        name="write_outputs",
    )(*results)


def solution(mesh):
    in_specs = (
        P("dp", "context", None),
        P("dp", "context", None),
        P("dp", None),
        P(None, "dp", "context"),
        P("context", "dp"),
        P(),
    )
    out_specs = (
        P("dp", "context", None),
        P("dp", "context", None),
        P(None, "dp", "context"),
        P("context", "dp"),
    )
    return jax.shard_map(
        on_device, mesh=mesh, in_specs=in_specs, out_specs=out_specs, check_vma=False
    )
```
